256 devices in a mesh: gx: 16 (over x, y), gy: 8 (over z), gz: 2 (over core).
Axes of the slice: x: 4, y: 4, z: 8, core: 2. Of those that a mesh axis runs over, the one named last changes fastest.
Arguments:
- right_side: float32 [16, 256, 2048], P('gz', 'gx', 'gy'), may hold values from -5 to 5
- conductivity: float32 [16, 256, 2048], P('gz', 'gx', 'gy'), may hold values from 0.1 to 10
- storage: float32 [16, 256, 2048], P('gz', 'gx', 'gy'), may hold values from 0.05 to 0.5
- basis: bfloat16 [8, 16, 256, 2048], P(None, 'gz', 'gx', 'gy'), may hold values from -1.25 to 1.25
Outputs:
- solution_field: float32 [16, 256, 2048], P('gz', 'gx', 'gy')
- residual: float32 [16, 256, 2048], P('gz', 'gx', 'gy')
- direction: float32 [16, 256, 2048], P('gz', 'gx', 'gy')
The draws below stay inside these ranges and needn't reach their ends.
All inputs are finite; a program needn't handle non-finite values.
Results may differ from the reference program's by a relative error of at most 0.0003.
Values may be sent and summed in bfloat16 or wider, within the bound.
No kernel may reach another device: no remote copies, remote signals or barrier semaphores. Data moves between devices by JAX's collectives and lax.ppermute only.
A program may use at most 64 MiB of HBM per device.

```python
import math
import jax
import jax.numpy as jnp
from jax import lax

CZ = 8
CX = 16
CY = 256
KITERS = 6
NZ = 16
NX = 256
NY = 2048
N_GX = 16
N_GY = 8
N_GZ = 2


def draw_right_side(key, part):
    key = jax.random.fold_in(key, 11)
    rough_key, wave_key, amp_key, phase_key = jax.random.split(key, 4)
    rough = jnp.clip(jax.random.normal(rough_key, (NZ, NX, NY), jnp.float32), -3.0, 3.0)
    freqs = jax.random.randint(wave_key, (4, 3), 1, 4).astype(jnp.float32)
    amplitudes = jax.random.uniform(amp_key, (4,), jnp.float32, 0.1, 0.25)
    phases = jax.random.uniform(phase_key, (4,), jnp.float32, -math.pi, math.pi)
    zcoord = ((jnp.arange(NZ, dtype=jnp.float32) + 0.5) / NZ)[:, None, None]
    xcoord = ((jnp.arange(NX, dtype=jnp.float32) + 0.5) / NX)[None, :, None]
    ycoord = ((jnp.arange(NY, dtype=jnp.float32) + 0.5) / NY)[None, None, :]
    smooth = jnp.zeros((NZ, NX, NY), jnp.float32)
    for number in range(4):
        angles = 2.0 * math.pi * (freqs[number, 0] * zcoord + freqs[number, 1] * xcoord + freqs[number, 2] * ycoord)
        smooth = smooth + amplitudes[number] * jnp.cos(angles + phases[number])
    return (rough + smooth).astype(jnp.float32)


def draw_basis(key, part):
    key = jax.random.fold_in(key, 23)
    noise = jax.random.uniform(key, (8, NZ, NX, NY), jnp.float32, -0.25, 0.25)
    zlocal = ((jnp.arange(NZ) % CZ).astype(jnp.float32) + 0.5) / CZ
    xlocal = ((jnp.arange(NX) % CX).astype(jnp.float32) + 0.5) / CX
    ylocal = ((jnp.arange(NY) % CY).astype(jnp.float32) + 0.5) / CY
    cosz = jnp.cos(math.pi * zlocal)[:, None, None]
    cosx = jnp.cos(math.pi * xlocal)[None, :, None]
    cosy = jnp.cos(math.pi * ylocal)[None, None, :]
    double_y = jnp.cos(2.0 * math.pi * ylocal)[None, None, :]
    shape = (NZ, NX, NY)
    modes = [jnp.ones(shape, jnp.float32), cosx, cosy, cosz, cosx * cosy, cosx * cosz, cosy * cosz, double_y]
    stacked = jnp.stack([jnp.broadcast_to(mode, shape) for mode in modes])
    return (stacked * (1.0 + noise)).astype(jnp.bfloat16)


def level_of(rng, shape, shards, least, top_value):
    level, own = 1.0, jax.random.fold_in(rng, 6)
    for dim, parts in shards:
        heights = jnp.exp(jax.random.uniform(jax.random.fold_in(own, dim), (parts,), jnp.float32, least / len(shards), top_value / len(shards)))
        level = level * jnp.repeat(heights, shape[dim] // parts).reshape([-1 if axis == dim else 1 for axis in range(len(shape))])
    return level


def setup_inputs(seed: int = 0) -> dict:
    key_of = jax.random.split(jax.random.key(seed), 5)
    return {
        "right_side": draw_right_side(jax.random.fold_in(key_of[4], 71), 0),
        "conductivity": jnp.clip(jnp.exp(math.log(10.0) - 4.6051702 * jax.random.uniform(key_of[1], (NZ, NX, NY), jnp.float32) ** level_of(key_of[1], (NZ, NX, NY), ((0, 2), (1, 16), (2, 8)), -0.2, 0.2)), 0.1, 10.0),
        "storage": jnp.clip(jnp.exp(math.log(0.5) - 2.3025851 * jax.random.uniform(key_of[2], (NZ, NX, NY), jnp.float32) ** level_of(key_of[2], (NZ, NX, NY), ((0, 2), (1, 16), (2, 8)), -0.2, 0.2)), 0.05, 0.5),
        "basis": draw_basis(jax.random.fold_in(key_of[4], 71), 0),
    }


HIGHEST = lax.Precision.HIGHEST
RELAXATION = 0.6


def neighbours(padded):
    return [padded[..., :-2, 1:-1, 1:-1], padded[..., 2:, 1:-1, 1:-1],
            padded[..., 1:-1, :-2, 1:-1], padded[..., 1:-1, 2:, 1:-1],
            padded[..., 1:-1, 1:-1, :-2], padded[..., 1:-1, 1:-1, 2:]]


def pad_cells(field):
    widths = [(0, 0)] * (field.ndim - 3) + [(1, 1)] * 3
    return jnp.pad(field, widths)


def harmonic(conductivity, padded):
    return [2.0 * conductivity * other / (conductivity + other) for other in neighbours(padded)]


def stencil(field, padded, weights, diagonal):
    total = diagonal * field
    for weight, other in zip(weights, neighbours(padded)):
        total = total - weight * other
    return total


def diagonal_tile(basis_block, weights, diagonal):
    basis_float = basis_block.astype(jnp.float32)
    image = stencil(basis_float, pad_cells(basis_float), weights, diagonal)
    return jnp.einsum("aijk,bijk->ab", basis_float, image, precision=HIGHEST)


def face_tile(weight_face, own_face, other_face):
    return -jnp.einsum("...ij,...aij,...bij->...ab", weight_face, own_face.astype(jnp.float32),
                       other_face.astype(jnp.float32), precision=HIGHEST)


def shift_grid(values, axis, from_lower):
    length = values.shape[axis]
    widths = [(0, 0)] * values.ndim
    widths[axis] = (1, 0) if from_lower else (0, 1)
    padded = jnp.pad(values, widths)
    offset = 0 if from_lower else 1
    return lax.slice_in_dim(padded, offset, offset + length, axis=axis)


def coarse_apply(tiles, values):
    near = [values, shift_grid(values, 2, True), shift_grid(values, 2, False),
            shift_grid(values, 0, True), shift_grid(values, 0, False),
            shift_grid(values, 1, True), shift_grid(values, 1, False)]
    stacked = jnp.stack(near, axis=-2)
    return jnp.einsum("...oab,...ob->...a", tiles, stacked, precision=HIGHEST)


def coarse_solve(tiles, source):
    solution = jnp.zeros_like(source)
    remainder = source
    search = source
    current = jnp.sum(remainder * remainder)
    for iteration in range(KITERS):
        image = coarse_apply(tiles, search)
        step_size = current / jnp.sum(search * image)
        solution = solution + step_size * search
        remainder = remainder - step_size * image
        updated = jnp.sum(remainder * remainder)
        search = remainder + (updated / current) * search
        current = updated
    return solution


def to_blocks(field):
    leading = field.shape[:-3]
    count = len(leading)
    shaped = field.reshape(leading + (N_GZ, CZ, N_GX, CX, N_GY, CY))
    order = (count + 2, count + 4, count) + tuple(range(count)) + (count + 1, count + 3, count + 5)
    return shaped.transpose(order)


def from_blocks(blocks):
    return blocks.transpose(2, 3, 0, 4, 1, 5).reshape(N_GZ * CZ, N_GX * CX, N_GY * CY)


def layer(values, axis, last):
    return lax.index_in_dim(values, values.shape[axis] - 1 if last else 0, axis, keepdims=False)


def all_tiles(basis_blocks, weights, diagonal):
    weight_blocks = [to_blocks(weight) for weight in weights]
    diagonal_blocks = to_blocks(diagonal)

    def per_slab(items):
        return jax.vmap(jax.vmap(diagonal_tile))(items[0], items[1], items[2])

    tiles = [lax.map(per_slab, (basis_blocks, weight_blocks, diagonal_blocks))]
    directions = [(0, False, 2), (0, True, 2), (1, False, 0), (1, True, 0), (2, False, 1), (2, True, 1)]
    for number, (cell_dim, own_last, block_axis) in enumerate(directions):
        own_face = layer(basis_blocks, 4 + cell_dim, own_last)
        other_face = shift_grid(layer(basis_blocks, 4 + cell_dim, not own_last), block_axis, not own_last)
        weight_face = layer(weight_blocks[number], 3 + cell_dim, own_last)
        tiles.append(face_tile(weight_face, own_face, other_face))
    return jnp.stack(tiles, axis=3)


def restrict(basis_blocks, field):
    def per_slab(items):
        return jnp.einsum("yzaijk,yzijk->yza", items[0].astype(jnp.float32), items[1], precision=HIGHEST)
    return lax.map(per_slab, (basis_blocks, to_blocks(field)))


def prolong(basis_blocks, values):
    def per_slab(items):
        return jnp.einsum("yzaijk,yza->yzijk", items[0].astype(jnp.float32), items[1], precision=HIGHEST)
    return from_blocks(lax.map(per_slab, (basis_blocks, values)))


def precondition(field, weights, diagonal, basis_blocks, tiles):
    first = RELAXATION * field / diagonal
    second = first + RELAXATION * (field - stencil(first, pad_cells(first), weights, diagonal)) / diagonal
    coarse = coarse_solve(tiles, restrict(basis_blocks, field))
    return second + prolong(basis_blocks, coarse)


def reference(right_side, conductivity, storage, basis):
    weights = harmonic(conductivity, pad_cells(conductivity))
    diagonal = storage + sum(weights)
    basis_blocks = to_blocks(basis)
    tiles = all_tiles(basis_blocks, weights, diagonal)
    preconditioned = precondition(right_side, weights, diagonal, basis_blocks, tiles)
    image = stencil(preconditioned, pad_cells(preconditioned), weights, diagonal)
    inner_first = jnp.sum(right_side * preconditioned)
    curvature = jnp.sum(preconditioned * image)
    step_size = inner_first / curvature
    solution_field = step_size * preconditioned
    residual = right_side - step_size * image
    refined = precondition(residual, weights, diagonal, basis_blocks, tiles)
    growth = jnp.sum(residual * refined) / inner_first
    direction = refined + growth * preconditioned
    return solution_field, residual, direction
```

```python
import functools

import jax
import jax.numpy as jnp
from jax import lax
from jax.experimental import pallas as pl
from jax.experimental.pallas import tpu as pltpu
from jax.sharding import PartitionSpec as P

KITERS = 6
RELAXATION = 0.6
HIGHEST = lax.Precision.HIGHEST
AXES = ("gx", "gy", "gz")
CZ, CX, CY = 8, 16, 256
EZ, EX, EY = 12, 24, 384
NDEV = 256
PAIRS = [(a, b) for a in range(8) for b in range(a, 8)]
ROW_Z, ROW_Y, ROW_X, ROW_OWN, ROW_RS, ROW_SAS, ROW_G, ROW_H = 0, 64, 128, 192, 228, 229, 232, 240
VMEM_LIMIT = 48 * 1024 * 1024


def harmonic(k, other):
    return 2.0 * k * other / jnp.maximum(k + other, 1e-30)


def y_next(v):
    return pltpu.roll(v, v.shape[1] - 1, 1)


def y_prev(v):
    return pltpu.roll(v, 1, 1)


def x_next(v):
    return pltpu.roll(v, v.shape[0] - 1, 0)


def x_prev(v):
    return pltpu.roll(v, 1, 0)


def apply_at(z, v, v_up, v_down, diag, wx, wy, wz_up, wz_down):
    total = diag * v - wy * y_next(v) - y_prev(wy * v) - wx * x_next(v) - x_prev(wx * v)
    if v_up is not None:
        total = total - wz_up * v_up
    if v_down is not None:
        total = total - wz_down * v_down
    return total


def fold(v):
    return (v[:8, :128] + v[8:, :128]) + (v[:8, 128:] + v[8:, 128:])


def prepare_kernel(f_ref, b_ref, xa_ref, xb_ref, ya_ref, yb_ref, kx_ref, ky_ref,
                   pay_ref, wx_ref, wy_ref, wz_ref, dg_ref, iv_ref, s_ref, u_ref,
                   first_ref, acc_ref):
    acc_ref[...] = jnp.zeros_like(acc_ref)
    for z in range(11):
        k = f_ref[0, z]
        wy_ref[z] = harmonic(k, y_next(k))
        wx_ref[z] = harmonic(k, x_next(k))
        wz_ref[z] = harmonic(k, f_ref[0, z + 1])
    for z in range(11):
        wy, wx = wy_ref[z], wx_ref[z]
        diag = f_ref[1, z] + wy + y_prev(wy) + wx + x_prev(wx) + wz_ref[z]
        if z:
            diag = diag + wz_ref[z - 1]
        inverse = RELAXATION / jnp.maximum(diag, 1e-3)
        dg_ref[z] = diag
        iv_ref[z] = inverse
        first_ref[z] = inverse * f_ref[2, z]

    def at(z, ref):
        return apply_at(z, ref[z], ref[z + 1], ref[z - 1] if z else None, dg_ref[z], wx_ref[z],
                        wy_ref[z], wz_ref[z], wz_ref[z - 1] if z else None)

    for z in range(10):
        s_ref[z] = first_ref[z] + iv_ref[z] * (f_ref[2, z] - at(z, first_ref))
    for z in range(9):
        u_ref[z] = at(z, s_ref)

    rows = lax.broadcasted_iota(jnp.int32, (CX, CY), 0)
    lanes = lax.broadcasted_iota(jnp.int32, (CX, CY), 1)

    def add(row, value):
        acc_ref[8 * row:8 * row + 8, :] += value

    def own(ref, *lead):
        return ref[lead + (slice(0, CX), slice(0, CY))]

    def body(z, carry):
        r, s, u = own(f_ref, 2, z), own(s_ref, z), own(u_ref, z)
        diag = own(dg_ref, z)
        wy = jnp.where(lanes == CY - 1, 0.0, own(wy_ref, z))
        wx = jnp.where(rows == CX - 1, 0.0, own(wx_ref, z))
        up = jnp.minimum(z + 1, CZ - 1)
        down = jnp.maximum(z - 1, 0)
        wz_up = jnp.where(z < CZ - 1, own(wz_ref, z), 0.0)
        wz_down = jnp.where(z > 0, own(wz_ref, down), 0.0)
        add(ROW_RS, fold(r * s))
        add(ROW_SAS, fold(s * u))
        basis = [own(b_ref, a, z) for a in range(8)]
        for b in range(8):
            add(ROW_G + b, fold(basis[b] * r))
            add(ROW_H + b, fold(basis[b] * u))
            image = apply_at(z, basis[b], own(b_ref, b, up), own(b_ref, b, down), diag, wx, wy,
                             wz_up, wz_down)
            for a in range(b + 1):
                add(ROW_OWN + PAIRS.index((a, b)), fold(basis[a] * image))
        return carry

    lax.fori_loop(0, CZ, body, 0)

    wz_face = -own(wz_ref, CZ - 1)
    wx_face = -harmonic(kx_ref[0], kx_ref[1])
    wy_face = -harmonic(ky_ref[0], ky_ref[1])
    for a in range(8):
        za = wz_face * own(b_ref, a, CZ - 1)
        xa = wx_face * xa_ref[a]
        ya = wy_face * ya_ref[a]
        for b in range(8):
            row = 8 * b + a
            add(ROW_Z + row, fold(za * own(b_ref, b, CZ)))
            x = xa * xb_ref[b]
            add(ROW_X + row, x[:, :128] + x[:, 128:])
            acc_ref[8 * (ROW_Y + row):8 * (ROW_Y + row) + 8, 0:CX] = ya * yb_ref[b]

    total = acc_ref[pl.ds(0, 256, stride=8), :]
    for sub in range(1, 8):
        total = total + acc_ref[pl.ds(sub, 256, stride=8), :]
    summed = lax.dot_general(jnp.ones((8, 128), jnp.float32), total, (((1,), (1,)), ((), ())),
                             precision=HIGHEST, preferred_element_type=jnp.float32)
    pay_ref[...] = summed[0:1]


def total_of(v):
    return jnp.sum(jnp.sum(v, axis=1, keepdims=True), axis=0, keepdims=True)


def coarse_solve(tile_ref, lane_even):
    def partner(c):
        return jnp.where(lane_even, pltpu.roll(c, NDEV - 1, 1), pltpu.roll(c, 1, 1))

    def apply_e(c):
        shifted = [c, partner(c), pltpu.roll(c, NDEV - 2, 1), pltpu.roll(c, NDEV - 16, 1),
                   pltpu.roll(c, 2, 1), pltpu.roll(c, 16, 1)]
        total = None
        for o, v in enumerate(shifted):
            part = None
            for b in range(8):
                tile = (tile_ref[8 * (8 * o + b):8 * (8 * o + b) + 8, :])
                term = tile * v[b:b + 1, :]
                part = term if part is None else part + term
            total = part if total is None else total + part
        return total

    def solve(g):
        remainder, search, current = g, g, total_of(g * g)
        solution = jnp.zeros_like(g)
        for _ in range(KITERS):
            image = apply_e(search)
            step = current / total_of(search * image)
            solution = solution + step * search
            remainder = remainder - step * image
            updated = total_of(remainder * remainder)
            search = remainder + (updated / current) * search
            current = updated
        return solution

    return apply_e, solve


def coarse_kernel(dev_ref, gath_ref, f_ref, b_ref, wx_ref, wy_ref, wz_ref, dg_ref, iv_ref, s_ref, u_ref,
                  sol_ref, res_ref, pre_ref, refined_ref, part_ref, scal_ref,
                  t_ref, tile_ref, pc_ref, q_ref):
    dev = dev_ref[0]
    gz = lax.rem(dev, 2)
    turned = gath_ref[...].T
    t_ref[0] = turned[:, :128]
    t_ref[1] = turned[:, 128:]

    def rows_at(index):
        return jnp.concatenate([t_ref[0, index, :], t_ref[1, index, :]], axis=1)

    for b in range(8):
        for a in range(8):
            row = ROW_OWN + PAIRS.index((min(a, b), max(a, b)))
            tile_ref[8 * b + a:8 * b + a + 1, :] = turned[row:row + 1, :]
    tile_ref[64:256, :] = turned[0:192, :]
    for b in range(8):
        tile_ref[256 + 8 * b:264 + 8 * b, :] = pltpu.roll(rows_at(pl.ds(ROW_Y + b, 8, stride=8)), 2, 1)
        tile_ref[320 + 8 * b:328 + 8 * b, :] = pltpu.roll(rows_at(pl.ds(ROW_X + b, 8, stride=8)), 16, 1)
    lane = lax.broadcasted_iota(jnp.int32, (8, NDEV), 1)
    apply_e, solve = coarse_solve(tile_ref, lax.rem(lane, 2) == 0)
    g = turned[ROW_G:ROW_G + 8]
    h = turned[ROW_H:ROW_H + 8]
    rs = turned[ROW_RS:ROW_RS + 1]
    sas = turned[ROW_SAS:ROW_SAS + 1]
    c1 = solve(g)
    ec1 = apply_e(c1)
    rz = total_of(rs) + total_of(g * c1)
    curvature = total_of(sas) + total_of((2.0 * h + ec1) * c1)
    step = rz / curvature
    g2 = g - step * (h + ec1)
    c2 = solve(g2)
    g2c2 = total_of(g2 * c2)

    own_c = pltpu.roll(c1, lax.rem(NDEV - dev, NDEV), 1)
    other = dev + 1 - 2 * gz
    other_c = pltpu.roll(c1, lax.rem(NDEV - other, NDEV), 1)
    row = lax.broadcasted_iota(jnp.int32, (EX, EY), 0)
    col = lax.broadcasted_iota(jnp.int32, (EX, EY), 1)
    col_own, col_high = col < CY, col < CY + 64
    row_own, row_high = row < CX, row < CX + 4

    def field_of(c, b):
        def at(lane_index):
            lane_index %= NDEV
            return c[b:b + 1, lane_index:lane_index + 1]

        def along_y(base):
            return jnp.where(col_own, at(base), jnp.where(col_high, at(base + 2), at(base - 2)))

        return jnp.where(row_own, along_y(0), jnp.where(row_high, along_y(16), along_y(-16)))

    for b in range(8):
        mine = field_of(own_c, b)
        theirs = field_of(other_c, b)
        for z in range(10):
            value = b_ref[b, z] * (mine if z < CZ else theirs)
            if b:
                value = value + pc_ref[z]
            pc_ref[z] = value

    def at(z, ref):
        return apply_at(z, ref[z], ref[z + 1], ref[z - 1] if z else None, dg_ref[z], wx_ref[z],
                        wy_ref[z], wz_ref[z], wz_ref[z - 1] if z else None)

    def out_z(z):
        return z + gz * (CZ - 1 - 2 * z)

    def keep(ref, z, value):
        ref[pl.ds(out_z(z), 1)] = value[None, :CX, :CY]

    for z in range(9):
        image = u_ref[z] + at(z, pc_ref)
        residual = f_ref[2, z] - step * image
        q_ref[z] = iv_ref[z] * residual
        if z < CZ:
            keep(res_ref, z, residual)
            pre = s_ref[z, :CX, :CY] + pc_ref[z, :CX, :CY]
            keep(pre_ref, z, pre)
            keep(sol_ref, z, step * pre)
    own_c2 = pltpu.roll(c2, lax.rem(NDEV - dev, NDEV), 1)
    partial = jnp.zeros((8, 128), jnp.float32)
    for z in range(CZ):
        residual = res_ref[pl.ds(out_z(z), 1)][0]
        second = q_ref[z, :CX, :CY] + iv_ref[z, :CX, :CY] * (residual - at(z, q_ref)[:CX, :CY])
        partial = partial + fold(residual * second)
        for b in range(8):
            second = second + b_ref[b, z, :CX, :CY] * own_c2[b:b + 1, 0:1]
        keep(refined_ref, z, second)
    part_ref[...] = jnp.sum(partial, axis=0, keepdims=True)
    spot = lax.broadcasted_iota(jnp.int32, (1, 128), 1)
    scal_ref[...] = jnp.where(spot == 0, g2c2, rz)


def finish_kernel(parts_ref, scal_ref, refined_ref, pre_ref, out_ref):
    growth = (total_of(parts_ref[...]) + scal_ref[:, 0:1]) / scal_ref[:, 1:2]
    for z in range(CZ):
        out_ref[z] = refined_ref[z] + growth * pre_ref[z]


def call(kernel, out_shapes, scratch, n_args, smem_first=False):
    whole = pl.BlockSpec(memory_space=pltpu.VMEM)
    specs = [whole] * n_args
    if smem_first:
        specs[0] = pl.BlockSpec(memory_space=pltpu.SMEM)
    return pl.pallas_call(
        kernel,
        out_shape=[jax.ShapeDtypeStruct(s, jnp.float32) for s in out_shapes],
        in_specs=specs,
        out_specs=[whole] * len(out_shapes),
        scratch_shapes=[pltpu.VMEM(s, jnp.float32) for s in scratch],
        compiler_params=pltpu.CompilerParams(vmem_limit_bytes=VMEM_LIMIT),
    )


def ring(axis, to):
    n = lax.axis_size(axis)
    return [(i, (i + to) % n) for i in range(n)]


def gather_rows(row):
    rows = jnp.broadcast_to(row[None], (NDEV,) + row.shape)
    return lax.all_to_all(rows, AXES, 0, 0, tiled=False).reshape(NDEV, row.shape[-1])


def local(right_side, conductivity, storage, basis):
    gx, gy, gz = (lax.axis_index(a) for a in AXES)
    dev = (gx * 8 + gy) * 2 + gz
    fields = jnp.stack([conductivity, storage, right_side])
    fields = jnp.where(gz == 0, fields, fields[:, ::-1])
    basis = jnp.where(gz == 0, basis, basis[:, ::-1])
    only_k = (jnp.arange(3) == 0)[:, None, None, None]

    def halo(v, axis, dim, width):
        low = lax.ppermute(lax.slice_in_dim(v, v.shape[dim] - width, None, axis=dim), axis, ring(axis, 1))
        high = lax.ppermute(lax.slice_in_dim(v, 0, width, axis=dim), axis, ring(axis, -1))
        return low, high

    def clear(low, high, index, count):
        low = jnp.where(only_k & (index == 0), 0.0, low)
        high = jnp.where(only_k & (index == count - 1), 0.0, high)
        return low, high

    fx_low, fx_high = clear(*halo(fields, "gx", 2, 4), gx, 16)
    bx_low, bx_high = halo(basis, "gx", 2, 2)
    xa = basis[:, :, CX - 1].astype(jnp.float32)
    xb = bx_high[:, :, 0].astype(jnp.float32)
    kx = jnp.stack([fields[0, :, CX - 1], fx_high[0, :, 0]])
    fields_x = jnp.concatenate([fields, fx_high, fx_low], axis=2)
    gap = jnp.zeros(basis.shape[:2] + (4,) + basis.shape[3:], basis.dtype)
    basis_x = jnp.concatenate([basis, bx_high, gap, bx_low], axis=2)

    fy_low, fy_high = clear(*halo(fields_x, "gy", 3, 4), gy, 8)
    by_low, by_high = halo(basis_x, "gy", 3, 2)
    ya = basis[:, :, :, CY - 1].astype(jnp.float32)
    yb = by_high[:, :, :CX, 0].astype(jnp.float32)
    ky = jnp.stack([fields[0, :, :, CY - 1], fy_high[0, :, :CX, 0]])
    fields_y = jnp.concatenate([fields_x, fy_high, jnp.ones((3, CZ, EX, EY - CY - 8), jnp.float32), fy_low], axis=3)
    basis_y = jnp.concatenate(
        [basis_x, by_high, jnp.zeros((8, CZ, EX, EY - CY - 4), basis.dtype), by_low], axis=3)

    swap = [(0, 1), (1, 0)]
    fz = lax.ppermute(fields_y[:, 4:], "gz", swap)
    bz = lax.ppermute(basis_y[:, 6:], "gz", swap)
    fields_e = jnp.concatenate([fields_y, fz[:, ::-1]], axis=1)
    basis_e = jnp.concatenate([basis_y, bz[:, ::-1]], axis=1).astype(jnp.float32)

    ext = (EZ, EX, EY)
    pay, wx, wy, wz, dg, iv, s, u = call(
        prepare_kernel, [(1, 256)] + [ext] * 7, [ext, (2048, 128)], 8
    )(fields_e, basis_e, xa, xb, ya, yb, kx, ky)
    gathered = gather_rows(pay)
    box = (CZ, CX, CY)
    sol, res, pre, refined, part, scal = call(
        coarse_kernel, [box] * 4 + [(1, 128)] * 2,
        [(2, 256, 128), (384, 256), ext, ext], 11, True,
    )(dev.astype(jnp.int32).reshape(1), gathered, fields_e, basis_e, wx, wy, wz, dg, iv, s, u)
    parts = gather_rows(part)
    direction, = call(finish_kernel, [box], [], 4)(parts, scal, refined, pre)
    return sol, res, direction


def solution(mesh):
    spec = P("gz", "gx", "gy")
    return jax.shard_map(
        local,
        mesh=mesh,
        in_specs=(spec, spec, spec, P(None, "gz", "gx", "gy")),
        out_specs=(spec, spec, spec),
        check_vma=False,
    )
```

```python
import functools

import jax
import jax.numpy as jnp
from jax import lax
from jax.experimental import pallas as pl
from jax.experimental.pallas import tpu as pltpu
from jax.sharding import PartitionSpec as P

KITERS = 6
RELAXATION = 0.6
HIGHEST = lax.Precision.HIGHEST
AXES = ("gx", "gy", "gz")
CZ, CX, CY = 8, 16, 256
EZ, EX, EY = 12, 24, 384
NDEV = 256
PAIRS = [(a, b) for a in range(8) for b in range(a, 8)]
ROW_Z, ROW_Y, ROW_X, ROW_OWN, ROW_RS, ROW_SAS, ROW_G, ROW_H = 0, 64, 128, 192, 228, 229, 232, 240
X_ROWS = 26
ST_LANE, R_LANE, FACE_LANE = 32, 56, 80
VMEM_LIMIT = 24 * 1024 * 1024


def harmonic(k, other):
    return 2.0 * k * other / jnp.maximum(k + other, 1e-30)


def y_next(v):
    return pltpu.roll(v, v.shape[1] - 1, 1)


def y_prev(v):
    return pltpu.roll(v, 1, 1)


def x_next(v):
    return pltpu.roll(v, v.shape[0] - 1, 0)


def x_prev(v):
    return pltpu.roll(v, 1, 0)


def apply_at(z, v, v_up, v_down, diag, wx, wy, wz_up, wz_down):
    total = diag * v - wy * y_next(v) - y_prev(wy * v) - wx * x_next(v) - x_prev(wx * v)
    if v_up is not None:
        total = total - wz_up * v_up
    if v_down is not None:
        total = total - wz_down * v_down
    return total


def fold(v):
    return (v[:8, :128] + v[8:, :128]) + (v[:8, 128:] + v[8:, 128:])


def pack_x_kernel(pos_ref, k_ref, st_ref, r_ref, b_ref, hi_ref, lo_ref, q_ref):
    gz = pos_ref[2]
    for z in range(CZ):
        src = z + gz * (CZ - 1 - 2 * z)
        base, j = X_ROWS * z, CZ - 1 - z
        k, st, r = (ref[pl.ds(src, 1)][0] for ref in (k_ref, st_ref, r_ref))
        hi_ref[base:base + 4, :] = k[12:16]
        lo_ref[base:base + 4, :] = k[0:4]
        hi_ref[base + 4:base + 7, :] = st[13:16]
        lo_ref[base + 4:base + 7, :] = st[0:3]
        hi_ref[base + 7:base + 10, :] = r[13:16]
        lo_ref[base + 7:base + 10, :] = r[0:3]
        if j < 4:
            q_ref[j] = k
        if j < 3:
            q_ref[4 + j] = st
            q_ref[7 + j] = r
        for a in range(8):
            v = b_ref[a, pl.ds(src, 1)][0].astype(jnp.float32)
            row = base + 10 + 2 * a
            hi_ref[row:row + 2, :] = v[14:16]
            lo_ref[row:row + 2, :] = v[0:2]
            if j < 2:
                q_ref[10 + 2 * a + j] = v


def flag(inside):
    return jnp.where(inside, 1.0, 0.0).astype(jnp.float32)


def pack_y_kernel(pos_ref, k_ref, st_ref, r_ref, b_ref, xh_ref, xl_ref, hi_ref, lo_ref, edge_ref):
    gx, gz = pos_ref[0], pos_ref[2]
    x_high, x_low = flag(gx < 15), flag(gx > 0)
    lane = lax.broadcasted_iota(jnp.int32, (EX, 128), 1)
    edge_ref[...] = jnp.ones_like(edge_ref)
    out = {}

    def put(side, half, tile, source, width, offset):
        rolled = pltpu.roll(tile, (offset - source) % 128, 1)
        mask = (lane >= offset) & (lane < offset + width)
        old = out.get((side, half), 0.0)
        out[side, half] = jnp.where(mask, rolled, old)

    def both(slot, main, half, base, width, offset, mul_h=None, mul_l=None):
        xh, xl = xh_ref[base:base + width, :], xl_ref[base:base + width, :]
        if mul_h is not None:
            xh, xl = xh * mul_h, xl * mul_l
        edge_ref[slot, 0:width, :] = xh
        edge_ref[slot, 8 - width:8, :] = xl
        full = jnp.concatenate([main, edge_ref[slot]], axis=0)
        put("hi", half, full[:, 128:], 128 - width, width, offset)
        put("lo", half, full[:, :128], 0, width, offset)
        return full

    for z in range(CZ):
        src = z + gz * (CZ - 1 - 2 * z)
        base = X_ROWS * z
        k, st, r = (ref[pl.ds(src, 1)][0] for ref in (k_ref, st_ref, r_ref))
        full = both(z, k, 0, base, 4, 4 * z, x_high, x_low)
        put("hi", 0, full[:, 128:], 127, 1, FACE_LANE + 2 * z + 1)
        put("lo", 0, full[:, :128], 0, 1, FACE_LANE + 2 * z + 1)
        both(8 + z, st, 0, base + 4, 3, ST_LANE + 3 * z)
        both(16 + z, r, 0, base + 7, 3, R_LANE + 3 * z)
        for a in range(8):
            v = b_ref[a, pl.ds(src, 1)][0].astype(jnp.float32)
            both(24 + 8 * a + z, v, 1, base + 10 + 2 * a, 2, 16 * a + 2 * z)
    for half in range(2):
        hi_ref[:, 128 * half:128 * half + 128] = out["hi", half]
        lo_ref[:, 128 * half:128 * half + 128] = out["lo", half]


def prepare_kernel(pos_ref, k_in, st_in, r_in, b_in, q_ref, xh_ref, xl_ref, xhq_ref, xlq_ref,
                   ys_ref, yh_ref, yl_ref, yhq_ref, ylq_ref,
                   pay_ref, r_ref, b_ref, wx_ref, wy_ref, wz_ref, dg_ref, iv_ref, s_ref, u_ref,
                   k_ref, st_ref, first_ref, acc_ref, xa_ref, xb_ref, wf_ref):
    gx, gy, gz = pos_ref[0], pos_ref[1], pos_ref[2]
    x_high, x_low = flag(gx < 15), flag(gx > 0)
    y_high, y_low = flag(gy < 7), flag(gy > 0)
    lane = lax.broadcasted_iota(jnp.int32, (EX, 128), 1)

    def assemble(ref, index, main, halos, base, width, half, offset, masked=False):
        xh, xl, yh, yl = halos
        xh, xl = xh[base:base + width, :], xl[base:base + width, :]
        columns = slice(128 * half, 128 * half + 128)
        yh = pltpu.roll(yh[:, columns], -offset % 128, 1)
        yl = pltpu.roll(yl[:, columns], (128 - width - offset) % 128, 1)
        if masked:
            xh, xl, yh, yl = xh * x_high, xl * x_low, yh * y_high, yl * y_low
        ref[index + (slice(0, CX), slice(0, CY))] = main
        if width < 4:
            ref[index + (slice(CX, EX), slice(0, CY))] = jnp.ones((8, CY), jnp.float32)
        ref[index + (slice(CX, CX + width), slice(0, CY))] = xh
        ref[index + (slice(EX - width, EX), slice(0, CY))] = xl
        ref[index + (slice(0, EX), slice(CY, EY))] = jnp.where(
            lane < width, yh, jnp.where(lane >= 128 - width, yl, 1.0))

    own_halos = (xh_ref, xl_ref, yh_ref, yl_ref)
    for z in range(CZ):
        src = z + gz * (CZ - 1 - 2 * z)
        base = X_ROWS * z
        assemble(k_ref, (z,), k_in[pl.ds(src, 1)][0], own_halos, base, 4, 0, 4 * z, True)
        assemble(st_ref, (z,), st_in[pl.ds(src, 1)][0], own_halos, base + 4, 3, 0, ST_LANE + 3 * z)
        assemble(r_ref, (z,), r_in[pl.ds(src, 1)][0], own_halos, base + 7, 3, 0, R_LANE + 3 * z)
        for a in range(8):
            v = b_in[a, pl.ds(src, 1)][0].astype(jnp.float32)
            assemble(b_ref, (a, z), v, own_halos, base + 10 + 2 * a, 2, 1, 16 * a + 2 * z)
    other_halos = (xhq_ref, xlq_ref, yhq_ref, ylq_ref)
    for j in range(4):
        z, theirs = CZ + j, CZ - 1 - j
        base = X_ROWS * (theirs - 4)
        assemble(k_ref, (z,), q_ref[j], other_halos, base, 4, 0, 4 * theirs, True)
        if j < 3:
            assemble(st_ref, (z,), q_ref[4 + j], other_halos, base + 4, 3, 0, ST_LANE + 3 * theirs)
            assemble(r_ref, (z,), q_ref[7 + j], other_halos, base + 7, 3, 0, R_LANE + 3 * theirs)
        if j < 2:
            for a in range(8):
                assemble(b_ref, (a, z), q_ref[10 + 2 * a + j], other_halos, base + 10 + 2 * a, 2, 1,
                         16 * a + 2 * theirs)

    acc_ref[...] = jnp.zeros_like(acc_ref)
    for z in range(11):
        k = k_ref[z]
        wy_ref[z] = harmonic(k, y_next(k))
        wx_ref[z] = harmonic(k, x_next(k))
        wz_ref[z] = harmonic(k, k_ref[z + 1])
    for z in range(11):
        wy, wx = wy_ref[z], wx_ref[z]
        diag = st_ref[z] + wy + y_prev(wy) + wx + x_prev(wx) + wz_ref[z]
        if z:
            diag = diag + wz_ref[z - 1]
        inverse = RELAXATION / jnp.maximum(diag, 1e-3)
        dg_ref[z] = diag
        iv_ref[z] = inverse
        first_ref[z] = inverse * r_ref[z]

    def at(z, ref):
        return apply_at(z, ref[z], ref[z + 1], ref[z - 1] if z else None, dg_ref[z], wx_ref[z],
                        wy_ref[z], wz_ref[z], wz_ref[z - 1] if z else None)

    for z in range(10):
        s_ref[z] = first_ref[z] + iv_ref[z] * (r_ref[z] - at(z, first_ref))
    for z in range(9):
        u_ref[z] = at(z, s_ref)

    rows = lax.broadcasted_iota(jnp.int32, (CX, CY), 0)
    lanes = lax.broadcasted_iota(jnp.int32, (CX, CY), 1)

    def add(row, value):
        acc_ref[8 * row:8 * row + 8, :] += value

    def own(ref, *lead):
        return ref[lead + (slice(0, CX), slice(0, CY))]

    def body(z, carry):
        r, s, u = own(r_ref, z), own(s_ref, z), own(u_ref, z)
        diag = own(dg_ref, z)
        wy = jnp.where(lanes == CY - 1, 0.0, own(wy_ref, z))
        wx = jnp.where(rows == CX - 1, 0.0, own(wx_ref, z))
        up = jnp.minimum(z + 1, CZ - 1)
        down = jnp.maximum(z - 1, 0)
        wz_up = jnp.where(z < CZ - 1, own(wz_ref, z), 0.0)
        wz_down = jnp.where(z > 0, own(wz_ref, down), 0.0)
        add(ROW_RS, fold(r * s))
        add(ROW_SAS, fold(s * u))
        basis = [own(b_ref, a, z) for a in range(8)]
        for b in range(8):
            add(ROW_G + b, fold(basis[b] * r))
            add(ROW_H + b, fold(basis[b] * u))
            image = apply_at(z, basis[b], own(b_ref, b, up), own(b_ref, b, down), diag, wx, wy,
                             wz_up, wz_down)
            for a in range(b + 1):
                add(ROW_OWN + PAIRS.index((a, b)), fold(basis[a] * image))
        return carry

    lax.fori_loop(0, CZ, body, 0)

    for z in range(CZ):
        wf_ref[z:z + 1, :] = -wx_ref[z, CX - 1:CX, 0:CY]
        for a in range(8):
            xa_ref[a, z:z + 1, :] = b_ref[a, z, CX - 1:CX, 0:CY]
            xb_ref[a, z:z + 1, :] = b_ref[a, z, CX:CX + 1, 0:CY]
    wz_face = -own(wz_ref, CZ - 1)
    wx_face = wf_ref[...]
    for a in range(8):
        za = wz_face * own(b_ref, a, CZ - 1)
        xa = wx_face * xa_ref[a]
        for b in range(8):
            row = 8 * b + a
            add(ROW_Z + row, fold(za * own(b_ref, b, CZ)))
            x = xa * xb_ref[b]
            add(ROW_X + row, x[:, :128] + x[:, 128:])

    lane = lax.broadcasted_iota(jnp.int32, (CX, 128), 1)
    weight = harmonic(ys_ref[0:CX, 0:128], yh_ref[0:CX, 0:128] * y_high)
    weight = pltpu.roll(weight, 128 - FACE_LANE, 1)
    weight = jnp.where((lane < 16) & (lax.rem(lane, 2) == 1), -weight, 0.0)
    for shift in (16, 32, 64):
        weight = weight + pltpu.roll(weight, shift, 1)
    mine = weight * ys_ref[0:CX, 128:256]
    theirs = pltpu.roll(yh_ref[0:CX, 128:256], 1, 1)
    group = lax.broadcasted_iota(jnp.int32, (8, 128), 1) // 16
    for d in range(8):
        product = mine * (pltpu.roll(theirs, 128 - 16 * d, 1) if d else theirs)
        product = product[:8] + product[8:]
        for a in range(8):
            row = 8 * (ROW_Y + 8 * ((a + d) % 8) + a)
            acc_ref[row:row + 8, :] = jnp.where(group == a, product, 0.0)

    total = acc_ref[pl.ds(0, 256, stride=8), :]
    for sub in range(1, 8):
        total = total + acc_ref[pl.ds(sub, 256, stride=8), :]
    summed = lax.dot_general(jnp.ones((8, 128), jnp.float32), total, (((1,), (1,)), ((), ())),
                             precision=HIGHEST, preferred_element_type=jnp.float32)
    pay_ref[0:1, :] = summed[0:1, :128]
    pay_ref[1:2, :] = summed[0:1, 128:]


def total_of(v):
    return jnp.sum(jnp.sum(v, axis=1, keepdims=True), axis=0, keepdims=True)


def coarse_solve(tile_ref, lane_even):
    def partner(c):
        return jnp.where(lane_even, pltpu.roll(c, NDEV - 1, 1), pltpu.roll(c, 1, 1))

    def apply_e(c):
        shifted = [c, partner(c), pltpu.roll(c, NDEV - 2, 1), pltpu.roll(c, NDEV - 16, 1),
                   pltpu.roll(c, 2, 1), pltpu.roll(c, 16, 1)]
        total = None
        for o, v in enumerate(shifted):
            part = None
            for b in range(8):
                tile = (tile_ref[8 * (8 * o + b):8 * (8 * o + b) + 8, :])
                term = tile * v[b:b + 1, :]
                part = term if part is None else part + term
            total = part if total is None else total + part
        return total

    def solve(g):
        remainder, search, current = g, g, total_of(g * g)
        solution = jnp.zeros_like(g)
        for _ in range(KITERS):
            image = apply_e(search)
            step = current / total_of(search * image)
            solution = solution + step * search
            remainder = remainder - step * image
            updated = total_of(remainder * remainder)
            search = remainder + (updated / current) * search
            current = updated
        return solution

    return apply_e, solve


def coarse_kernel(pos_ref, gath_ref, r_ref, b_ref, wx_ref, wy_ref, wz_ref, dg_ref, iv_ref, s_ref, u_ref,
                  sol_ref, res_ref, pre_ref, refined_ref, part_ref, scal_ref,
                  t_ref, tile_ref, pc_ref, q_ref):
    gz = pos_ref[2]
    dev = (pos_ref[0] * 8 + pos_ref[1]) * 2 + gz
    turned = gath_ref[...].T
    t_ref[0] = turned[:, :128]
    t_ref[1] = turned[:, 128:]

    def rows_at(index):
        return jnp.concatenate([t_ref[0, index, :], t_ref[1, index, :]], axis=1)

    for b in range(8):
        for a in range(8):
            row = ROW_OWN + PAIRS.index((min(a, b), max(a, b)))
            tile_ref[8 * b + a:8 * b + a + 1, :] = turned[row:row + 1, :]
    tile_ref[64:256, :] = turned[0:192, :]
    for b in range(8):
        tile_ref[256 + 8 * b:264 + 8 * b, :] = pltpu.roll(rows_at(pl.ds(ROW_Y + b, 8, stride=8)), 2, 1)
        tile_ref[320 + 8 * b:328 + 8 * b, :] = pltpu.roll(rows_at(pl.ds(ROW_X + b, 8, stride=8)), 16, 1)
    lane = lax.broadcasted_iota(jnp.int32, (8, NDEV), 1)
    apply_e, solve = coarse_solve(tile_ref, lax.rem(lane, 2) == 0)
    g = turned[ROW_G:ROW_G + 8]
    h = turned[ROW_H:ROW_H + 8]
    rs = turned[ROW_RS:ROW_RS + 1]
    sas = turned[ROW_SAS:ROW_SAS + 1]
    c1 = solve(g)
    ec1 = apply_e(c1)
    rz = total_of(rs) + total_of(g * c1)
    curvature = total_of(sas) + total_of((2.0 * h + ec1) * c1)
    step = rz / curvature
    g2 = g - step * (h + ec1)
    c2 = solve(g2)
    g2c2 = total_of(g2 * c2)

    own_c = pltpu.roll(c1, lax.rem(NDEV - dev, NDEV), 1)
    other = dev + 1 - 2 * gz
    other_c = pltpu.roll(c1, lax.rem(NDEV - other, NDEV), 1)
    row = lax.broadcasted_iota(jnp.int32, (EX, EY), 0)
    col = lax.broadcasted_iota(jnp.int32, (EX, EY), 1)
    col_own, col_high = col < CY, col < CY + 64
    row_own, row_high = row < CX, row < CX + 4

    def field_of(c, b):
        def at(lane_index):
            lane_index %= NDEV
            return c[b:b + 1, lane_index:lane_index + 1]

        def along_y(base):
            return jnp.where(col_own, at(base), jnp.where(col_high, at(base + 2), at(base - 2)))

        return jnp.where(row_own, along_y(0), jnp.where(row_high, along_y(16), along_y(-16)))

    for b in range(8):
        mine = field_of(own_c, b)
        theirs = field_of(other_c, b)
        for z in range(10):
            value = b_ref[b, z] * (mine if z < CZ else theirs)
            if b:
                value = value + pc_ref[z]
            pc_ref[z] = value

    def at(z, ref):
        return apply_at(z, ref[z], ref[z + 1], ref[z - 1] if z else None, dg_ref[z], wx_ref[z],
                        wy_ref[z], wz_ref[z], wz_ref[z - 1] if z else None)

    def out_z(z):
        return z + gz * (CZ - 1 - 2 * z)

    def keep(ref, z, value):
        ref[pl.ds(out_z(z), 1)] = value[None, :CX, :CY]

    for z in range(9):
        image = u_ref[z] + at(z, pc_ref)
        residual = r_ref[z] - step * image
        q_ref[z] = iv_ref[z] * residual
        if z < CZ:
            keep(res_ref, z, residual)
            pre = s_ref[z, :CX, :CY] + pc_ref[z, :CX, :CY]
            keep(pre_ref, z, pre)
            keep(sol_ref, z, step * pre)
    own_c2 = pltpu.roll(c2, lax.rem(NDEV - dev, NDEV), 1)
    partial = jnp.zeros((8, 128), jnp.float32)
    for z in range(CZ):
        residual = res_ref[pl.ds(out_z(z), 1)][0]
        second = q_ref[z, :CX, :CY] + iv_ref[z, :CX, :CY] * (residual - at(z, q_ref)[:CX, :CY])
        partial = partial + fold(residual * second)
        for b in range(8):
            second = second + b_ref[b, z, :CX, :CY] * own_c2[b:b + 1, 0:1]
        keep(refined_ref, z, second)
    part_ref[...] = jnp.sum(partial, axis=0, keepdims=True)
    spot = lax.broadcasted_iota(jnp.int32, (1, 128), 1)
    scal_ref[...] = jnp.where(spot == 0, g2c2, rz)


def finish_kernel(parts_ref, scal_ref, refined_ref, pre_ref, out_ref):
    growth = (total_of(parts_ref[...]) + scal_ref[:, 0:1]) / scal_ref[:, 1:2]
    for z in range(CZ):
        out_ref[z] = refined_ref[z] + growth * pre_ref[z]


def call(kernel, out_shapes, scratch, n_args, smem_first=False):
    whole = pl.BlockSpec(memory_space=pltpu.VMEM)
    specs = [whole] * n_args
    if smem_first:
        specs[0] = pl.BlockSpec(memory_space=pltpu.SMEM)
    return pl.pallas_call(
        kernel,
        out_shape=[jax.ShapeDtypeStruct(s, jnp.float32) for s in out_shapes],
        in_specs=specs,
        out_specs=[whole] * len(out_shapes),
        scratch_shapes=[pltpu.VMEM(s, jnp.float32) for s in scratch],
        compiler_params=pltpu.CompilerParams(vmem_limit_bytes=VMEM_LIMIT),
    )


def ring(axis, to):
    n = lax.axis_size(axis)
    return [(i, (i + to) % n) for i in range(n)]


def gather_rows(row):
    rows = jnp.broadcast_to(row[None], (NDEV,) + row.shape)
    return lax.all_to_all(rows, AXES, 0, 0, tiled=False)


def local(right_side, conductivity, storage, basis):
    pos = jnp.stack([lax.axis_index(a) for a in AXES]).astype(jnp.int32)
    fields = (conductivity, storage, right_side, basis)
    swap = [(0, 1), (1, 0)]

    def exchange(axis, hi, lo):
        return lax.ppermute(lo, axis, ring(axis, -1)), lax.ppermute(hi, axis, ring(axis, 1))

    faces = (X_ROWS * CZ, CY)
    hi, lo, layers = call(pack_x_kernel, [faces, faces, (X_ROWS, CX, CY)], [], 5, True)(pos, *fields)
    x_high, x_low = exchange("gx", hi, lo)
    other_layers = lax.ppermute(layers, "gz", swap)
    other_xh = lax.ppermute(x_high[X_ROWS * 4:], "gz", swap)
    other_xl = lax.ppermute(x_low[X_ROWS * 4:], "gz", swap)
    columns = (EX, 256)
    hi, lo = call(pack_y_kernel, [columns, columns], [(88, 8, CY)], 7, True)(pos, *fields, x_high, x_low)
    y_high, y_low = exchange("gy", hi, lo)
    other_yh = lax.ppermute(y_high, "gz", swap)
    other_yl = lax.ppermute(y_low, "gz", swap)

    ext = (EZ, EX, EY)
    pay, r, b, wx, wy, wz, dg, iv, s, u = call(
        prepare_kernel,
        [(2, 128), ext, (8, 10, EX, EY)] + [ext] * 7,
        [ext, ext, ext, (2048, 128), (8, CZ, CY), (8, CZ, CY), (CZ, CY)], 15, True,
    )(pos, *fields, other_layers, x_high, x_low, other_xh, other_xl, hi, y_high, y_low, other_yh, other_yl)
    gathered = gather_rows(pay).reshape(NDEV, 256)
    box = (CZ, CX, CY)
    sol, res, pre, refined, part, scal = call(
        coarse_kernel, [box] * 4 + [(1, 128)] * 2,
        [(2, 256, 128), (384, 256), ext, ext], 11, True,
    )(pos, gathered, r, b, wx, wy, wz, dg, iv, s, u)
    parts = gather_rows(part).reshape(NDEV, 128)
    direction, = call(finish_kernel, [box], [], 4)(parts, scal, refined, pre)
    return sol, res, direction


def solution(mesh):
    spec = P("gz", "gx", "gy")
    return jax.shard_map(
        local,
        mesh=mesh,
        in_specs=(spec, spec, spec, P(None, "gz", "gx", "gy")),
        out_specs=(spec, spec, spec),
        check_vma=False,
    )
```

```python
import functools

import jax
import jax.numpy as jnp
from jax import lax
from jax.experimental import pallas as pl
from jax.experimental.pallas import tpu as pltpu
from jax.sharding import PartitionSpec as P

KITERS = 6
RELAXATION = 0.6
HIGHEST = lax.Precision.HIGHEST
AXES = ("gx", "gy", "gz")
CZ, CX, CY = 8, 16, 256
EZ, EX, EY = 12, 24, 384
NDEV = 256
PAIRS = [(a, b) for a in range(8) for b in range(a, 8)]
ROW_Z, ROW_Y, ROW_X, ROW_OWN, ROW_RS, ROW_SAS, ROW_G, ROW_H = 0, 64, 128, 192, 228, 229, 232, 240
DEPTHS = (4, 3, 3)
STEPS = [(f, d) for f in range(3) for d in range(DEPTHS[f])]
FIELD_ROW, LAST_ROW, FACE_ROWS = 128, 208, 216
FACE_LANE, CORNER_LANE = 96, 40
VMEM_LIMIT = 24 * 1024 * 1024


def harmonic(k, other):
    return 2.0 * k * other / jnp.maximum(k + other, 1e-30)


def y_next(v):
    return pltpu.roll(v, v.shape[1] - 1, 1)


def y_prev(v):
    return pltpu.roll(v, 1, 1)


def x_next(v):
    return pltpu.roll(v, v.shape[0] - 1, 0)


def x_prev(v):
    return pltpu.roll(v, 1, 0)


def apply_at(z, v, v_up, v_down, diag, wx, wy, wz_up, wz_down):
    total = diag * v - wy * y_next(v) - y_prev(wy * v) - wx * x_next(v) - x_prev(wx * v)
    if v_up is not None:
        total = total - wz_up * v_up
    if v_down is not None:
        total = total - wz_down * v_down
    return total


def fold(v):
    return (v[:8, :128] + v[8:, :128]) + (v[:8, 128:] + v[8:, 128:])


def flag(inside):
    return jnp.where(inside, 1.0, 0.0).astype(jnp.float32)


def source_of(z, gz):
    return z + gz * (CZ - 1 - 2 * z)


def pack_x_kernel(pos_ref, f_ref, b_ref, hi_ref, lo_ref, small_hi_ref, small_lo_ref, q_ref):
    gz = pos_ref[2]
    for z in range(CZ):
        src, j = source_of(z, gz), CZ - 1 - z
        fields = [f_ref[f, pl.ds(src, 1)][0] for f in range(3)]
        for t, (f, d) in enumerate(STEPS):
            row = FIELD_ROW + 8 * t + z
            hi_ref[row:row + 1, :] = fields[f][CX - 1 - d:CX - d]
            lo_ref[row:row + 1, :] = fields[f][d:d + 1]
        if j < 4:
            q_ref[j] = fields[0]
        if j < 3:
            q_ref[4 + j] = fields[1]
            q_ref[7 + j] = fields[2]
        for a in range(8):
            v = b_ref[a, pl.ds(src, 1)][0]
            for d in range(2):
                row = 16 * a + 8 * d + z
                hi_ref[row:row + 1, :] = v[CX - 1 - d:CX - d]
                lo_ref[row:row + 1, :] = v[d:d + 1]
            if j == 0:
                hi_ref[LAST_ROW + a:LAST_ROW + a + 1, :] = v[CX - 1:CX]
                lo_ref[LAST_ROW + a:LAST_ROW + a + 1, :] = v[0:1]
            if j < 2:
                q_ref[10 + 2 * a + j] = v
    lane = lax.broadcasted_iota(jnp.int32, (8, 128), 1)
    rows = [FIELD_ROW + 8 * t for t in range(10)] + [16 * a for a in range(8)]
    for ref, small_ref in ((hi_ref, small_hi_ref), (lo_ref, small_lo_ref)):
        first = last = jnp.zeros((8, 128), jnp.float32)
        for i, row in enumerate(rows):
            mask = (lane >= 4 * i) & (lane < 4 * i + 4)
            first = jnp.where(mask, pltpu.roll(ref[row:row + 8, :128], 4 * i, 1), first)
            last = jnp.where(mask, pltpu.roll(ref[row:row + 8, 128:], 4 * i + 4, 1), last)
        small_ref[:, :128] = first
        small_ref[:, 128:] = last


def pack_y_kernel(pos_ref, f_ref, b_ref, hi_ref, lo_ref):
    gz = pos_ref[2]
    lane = lax.broadcasted_iota(jnp.int32, (CX, 128), 1)
    hi = [jnp.zeros((CX, 128), jnp.float32)] * 2
    lo = [jnp.zeros((CX, 128), jnp.float32)] * 2

    def put(half, v, width, offset):
        mask = (lane >= offset) & (lane < offset + width)
        hi[half] = jnp.where(mask, pltpu.roll(v[:, 128:], (offset + width) % 128, 1), hi[half])
        lo[half] = jnp.where(mask, pltpu.roll(v[:, :128], offset, 1), lo[half])

    for z in range(CZ):
        src = source_of(z, gz)
        for f in range(3):
            v = f_ref[f, pl.ds(src, 1)][0]
            put(0, v, 4, 32 * f + 4 * z)
            if f == 0:
                put(0, v, 1, FACE_LANE + 2 * z + 1)
        for a in range(8):
            put(1, b_ref[a, pl.ds(src, 1)][0], 2, 16 * a + 2 * z)
    for half in range(2):
        hi_ref[:, 128 * half:128 * half + 128] = hi[half]
        lo_ref[:, 128 * half:128 * half + 128] = lo[half]


def gram_kernel(pos_ref, f_ref, b_ref, part_ref):
    gz = pos_ref[2]
    part_ref[...] = jnp.zeros_like(part_ref)
    rows = lax.broadcasted_iota(jnp.int32, (CX, CY), 0)
    lanes = lax.broadcasted_iota(jnp.int32, (CX, CY), 1)

    def add(row, value):
        part_ref[8 * row:8 * row + 8, :] += value

    def body(z, carry):
        src, up, down = source_of(z, gz), jnp.minimum(z + 1, CZ - 1), jnp.maximum(z - 1, 0)
        k, st, r = (f_ref[f, pl.ds(src, 1)][0] for f in range(3))
        src_up, src_down = source_of(up, gz), source_of(down, gz)
        wy = jnp.where(lanes == CY - 1, 0.0, harmonic(k, y_next(k)))
        wx = jnp.where(rows == CX - 1, 0.0, harmonic(k, x_next(k)))
        wz_up = jnp.where(z < CZ - 1, harmonic(k, f_ref[0, pl.ds(src_up, 1)][0]), 0.0)
        wz_down = jnp.where(z > 0, harmonic(k, f_ref[0, pl.ds(src_down, 1)][0]), 0.0)
        diag = st + wy + y_prev(wy) + wx + x_prev(wx) + wz_up + wz_down
        basis = [b_ref[a, pl.ds(src, 1)][0] for a in range(8)]
        for b in range(8):
            add(36 + b, fold(basis[b] * r))
            image = apply_at(z, basis[b], b_ref[b, pl.ds(src_up, 1)][0],
                             b_ref[b, pl.ds(src_down, 1)][0], diag,
                             wx, wy, wz_up, wz_down)
            for a in range(b + 1):
                add(PAIRS.index((a, b)), fold(basis[a] * image))
        return carry

    lax.fori_loop(0, CZ, body, 0)


def prepare_kernel(pos_ref, f_in, part_ref, b_ref, q_ref, hi_ref, lo_ref, xh_ref, xl_ref, xhq_ref,
                   xlq_ref, ys_hi_ref, ys_lo_ref, yh_ref, yl_ref, yhq_ref, ylq_ref,
                   pay_ref, r_ref, wx_ref, wy_ref, wz_ref, dg_ref, iv_ref, s_ref, u_ref,
                   k_ref, st_ref, first_ref, acc_ref):
    gx, gy, gz = pos_ref[0], pos_ref[1], pos_ref[2]
    x_high, x_low = flag(gx < 15), flag(gx > 0)
    y_high, y_low = flag(gy < 7), flag(gy > 0)
    lane16 = lax.broadcasted_iota(jnp.int32, (CX, 128), 1)
    lane8 = lax.broadcasted_iota(jnp.int32, (8, 128), 1)
    outs = (k_ref, st_ref, r_ref)

    def beside(lane, high, low, offset, f):
        high = pltpu.roll(high, -offset % 128, 1)
        low = pltpu.roll(low, (124 - offset) % 128, 1)
        if f == 0:
            high, low = high * y_high, low * y_low
        return jnp.where(lane < 4, high, jnp.where(lane >= 124, low, 1.0))

    def main(f, z, value, high, low, layer):
        ref = outs[f]
        ref[z, :CX, :CY] = value
        ref[z, :CX, CY:] = beside(lane16, high[:CX, :128], low[:CX, :128], 32 * f + 4 * layer, f)
        if f:
            ref[z, CX:, :] = jnp.ones((EX - CX, EY), jnp.float32)

    def edges(t, sides, high, low, places):
        f, d = STEPS[t]
        for side, (ref, inside, row) in enumerate(sides):
            wide = ref[row + 8 * t:row + 8 * t + 8, :]
            columns = slice(128 * side, 128 * side + 128)
            corner = beside(lane8, high[CX:, columns], low[CX:, columns], 4 * t, f)
            if f == 0:
                wide, corner = wide * inside, corner * inside
            to = EX - 1 - d if side else CX + d
            for z, layer in places:
                outs[f][z, to:to + 1, :CY] = wide[layer:layer + 1]
                outs[f][z, to:to + 1, CY:] = corner[layer:layer + 1]

    high, low = yh_ref[...], yl_ref[...]
    for z in range(CZ):
        src = source_of(z, gz)
        for f in range(3):
            main(f, z, f_in[f, pl.ds(src, 1)][0], high, low, z)
    sides = ((xh_ref, x_high, FIELD_ROW), (xl_ref, x_low, FIELD_ROW))
    for t in range(len(STEPS)):
        edges(t, sides, high, low, [(z, z) for z in range(CZ)])
    high, low = yhq_ref[...], ylq_ref[...]
    first_layer = (0, 4, 7)
    for f in range(3):
        for j in range(DEPTHS[f]):
            main(f, CZ + j, q_ref[first_layer[f] + j], high, low, CZ - 1 - j)
    sides = ((xhq_ref, x_high, 0), (xlq_ref, x_low, 0))
    for t, (f, d) in enumerate(STEPS):
        edges(t, sides, high, low, [(CZ + j, CZ - 1 - j) for j in range(DEPTHS[f])])

    for z in range(11):
        k = k_ref[z]
        wy_ref[z] = harmonic(k, y_next(k))
        wx_ref[z] = harmonic(k, x_next(k))
        wz_ref[z] = harmonic(k, k_ref[z + 1])
    for z in range(11):
        wy, wx = wy_ref[z], wx_ref[z]
        diag = st_ref[z] + wy + y_prev(wy) + wx + x_prev(wx) + wz_ref[z]
        if z:
            diag = diag + wz_ref[z - 1]
        inverse = RELAXATION / jnp.maximum(diag, 1e-3)
        dg_ref[z] = diag
        iv_ref[z] = inverse
        first_ref[z] = inverse * r_ref[z]

    def at(z, ref):
        return apply_at(z, ref[z], ref[z + 1], ref[z - 1] if z else None, dg_ref[z], wx_ref[z],
                        wy_ref[z], wz_ref[z], wz_ref[z - 1] if z else None)

    for z in range(10):
        s_ref[z] = first_ref[z] + iv_ref[z] * (r_ref[z] - at(z, first_ref))
    for z in range(9):
        u_ref[z] = at(z, s_ref)

    def set_row(row, value):
        acc_ref[8 * row:8 * row + 8, :] = value

    def layers(products):
        total = None
        for z in range(CZ):
            total = products(z) if total is None else total + products(z)
        return fold(total)

    def own(ref, z):
        return ref[z, :CX, :CY]

    def basis(a, z):
        return b_ref[a, pl.ds(source_of(z, gz), 1)][0]

    acc_ref[8 * ROW_RS:8 * ROW_G, :] = jnp.zeros((8 * (ROW_G - ROW_RS), 128), jnp.float32)
    acc_ref[8 * (ROW_H + 8):2048, :] = jnp.zeros((2048 - 8 * (ROW_H + 8), 128), jnp.float32)
    set_row(ROW_RS, layers(lambda z: own(r_ref, z) * own(s_ref, z)))
    set_row(ROW_SAS, layers(lambda z: own(u_ref, z) * own(s_ref, z)))
    for a in range(8):
        set_row(ROW_H + a, layers(lambda z: basis(a, z) * own(u_ref, z)))
    acc_ref[8 * ROW_G:8 * (ROW_G + 8), :] = part_ref[8 * 36:8 * 44, :]

    odd = (lane16 < 16) & (lax.rem(lane16, 2) == 1)
    group = lane8 // 16

    def y_weight(own_ref, beside_ref, inside):
        weight = harmonic(own_ref[...][:CX, :128], beside_ref[...][:CX, :128] * inside)
        weight = jnp.where(odd, pltpu.roll(weight, 128 - FACE_LANE, 1), 0.0)
        for shift in (16, 32, 64):
            weight = weight + pltpu.roll(weight, shift, 1)
        return weight

    def turned(v, d):
        return pltpu.roll(v, 128 - 16 * d, 1) if d else v

    mine = ys_hi_ref[...][:CX, 128:]
    first_mine = pltpu.roll(ys_lo_ref[...][:CX, 128:], 1, 1)
    theirs = pltpu.roll(yh_ref[...][:CX, 128:], 1, 1)
    weighted = y_weight(ys_hi_ref, yh_ref, y_high) * mine
    first_weighted = y_weight(ys_lo_ref, yl_ref, y_low) * first_mine
    face_y = {}
    for d in range(8):
        product = -weighted * turned(theirs, d)
        product = product[:8] + product[8:]
        for a in range(8):
            set_row(ROW_Y + 8 * ((a + d) % 8) + a, jnp.where(group == a, product, 0.0))
        if d < 5:
            inner = weighted * turned(mine, d) + first_weighted * turned(first_mine, d)
            face_y[d] = inner[:8] + inner[8:]

    wz_face = own(wz_ref, CZ - 1)
    wx_face = harmonic(hi_ref[FIELD_ROW:FIELD_ROW + 8, :], xh_ref[FIELD_ROW:FIELD_ROW + 8, :] * x_high)
    wx_first = harmonic(lo_ref[FIELD_ROW:FIELD_ROW + 8, :], xl_ref[FIELD_ROW:FIELD_ROW + 8, :] * x_low)
    for a in range(8):
        za = wz_face * basis(a, CZ - 1)
        xa = wx_face * hi_ref[16 * a:16 * a + 8, :]
        xa_first = wx_first * lo_ref[16 * a:16 * a + 8, :]
        for b in range(8):
            row = 8 * b + a
            set_row(ROW_Z + row, -fold(za * q_ref[10 + 2 * b]))
            x = xa * xh_ref[16 * b:16 * b + 8, :]
            set_row(ROW_X + row, -(x[:, :128] + x[:, 128:]))
            if b < a:
                continue
            x = xa * hi_ref[16 * b:16 * b + 8, :] + xa_first * lo_ref[16 * b:16 * b + 8, :]
            pair = PAIRS.index((a, b))
            value = part_ref[8 * pair:8 * pair + 8, :] + fold(za * basis(b, CZ - 1)) + x[:, :128] + x[:, 128:]
            d, place = (b - a, a) if b - a < 5 else (a - b + 8, b)
            set_row(ROW_OWN + pair, value + jnp.where(group == place, face_y[d], 0.0))

    total = acc_ref[pl.ds(0, 256, stride=8), :]
    for sub in range(1, 8):
        total = total + acc_ref[pl.ds(sub, 256, stride=8), :]
    summed = lax.dot_general(jnp.ones((8, 128), jnp.float32), total, (((1,), (1,)), ((), ())),
                             precision=HIGHEST, preferred_element_type=jnp.float32)
    pay_ref[0:1, :] = summed[0:1, :128]
    pay_ref[1:2, :] = summed[0:1, 128:]


def total_of(v):
    v = jnp.sum(v, axis=0, keepdims=True)
    if v.shape[1] == 256:
        v = v[:, :128] + v[:, 128:]
    return jnp.sum(v, axis=1, keepdims=True)


def dot(left, right):
    v = left * right
    return total_of(v[:, :128] + v[:, 128:])


def coarse_solve(tile_ref, lane_even):
    def partner(c):
        return jnp.where(lane_even, pltpu.roll(c, NDEV - 1, 1), pltpu.roll(c, 1, 1))

    def apply_e(c):
        shifted = [c, partner(c), pltpu.roll(c, NDEV - 2, 1), pltpu.roll(c, NDEV - 16, 1),
                   pltpu.roll(c, 2, 1), pltpu.roll(c, 16, 1)]
        total = None
        for o, v in enumerate(shifted):
            part = None
            for b in range(8):
                tile = (tile_ref[8 * (8 * o + b):8 * (8 * o + b) + 8, :])
                term = tile * v[b:b + 1, :]
                part = term if part is None else part + term
            total = part if total is None else total + part
        return total

    def solve(g):
        remainder, search, image = g, g, apply_e(g)
        current, along = dot(g, g), dot(g, image)
        solution = jnp.zeros_like(g)
        for iteration in range(KITERS):
            step = current / along
            solution = solution + step * search
            remainder = remainder - step * image
            if iteration == KITERS - 1:
                break
            applied = apply_e(remainder)
            updated = dot(remainder, remainder)
            ratio = updated / current
            along = dot(remainder, applied) + ratio * (2.0 * dot(remainder, image) + ratio * along)
            search = remainder + ratio * search
            image = applied + ratio * image
            current = updated
        return solution, g - remainder

    return solve


def coarse_kernel(pos_ref, gath_ref, r_ref, b_ref, q_in, xh_ref, xl_ref, xhq_ref, xlq_ref,
                  yh_ref, yl_ref, yhq_ref, ylq_ref, wx_ref, wy_ref, wz_ref, dg_ref, iv_ref, s_ref, u_ref,
                  sol_ref, res_ref, pre_ref, refined_ref, part_ref, scal_ref,
                  t_ref, tile_ref, pc_ref, q_ref):
    gz = pos_ref[2]
    dev = (pos_ref[0] * 8 + pos_ref[1]) * 2 + gz
    turned = gath_ref[...].T
    t_ref[0] = turned[:, :128]
    t_ref[1] = turned[:, 128:]

    def rows_at(index):
        return jnp.concatenate([t_ref[0, index, :], t_ref[1, index, :]], axis=1)

    for b in range(8):
        for a in range(8):
            row = ROW_OWN + PAIRS.index((min(a, b), max(a, b)))
            tile_ref[8 * b + a:8 * b + a + 1, :] = turned[row:row + 1, :]
    tile_ref[64:256, :] = turned[0:192, :]
    for b in range(8):
        tile_ref[256 + 8 * b:264 + 8 * b, :] = pltpu.roll(rows_at(pl.ds(ROW_Y + b, 8, stride=8)), 2, 1)
        tile_ref[320 + 8 * b:328 + 8 * b, :] = pltpu.roll(rows_at(pl.ds(ROW_X + b, 8, stride=8)), 16, 1)
    lane = lax.broadcasted_iota(jnp.int32, (8, NDEV), 1)
    solve = coarse_solve(tile_ref, lax.rem(lane, 2) == 0)
    g = turned[ROW_G:ROW_G + 8]
    h = turned[ROW_H:ROW_H + 8]
    rs = turned[ROW_RS:ROW_RS + 1]
    sas = turned[ROW_SAS:ROW_SAS + 1]
    c1, ec1 = solve(g)
    rz = total_of(rs) + dot(g, c1)
    curvature = total_of(sas) + dot(2.0 * h + ec1, c1)
    step = rz / curvature
    g2 = g - step * (h + ec1)
    c2, _ = solve(g2)
    g2c2 = dot(g2, c2)

    own_c = pltpu.roll(c1, lax.rem(NDEV - dev, NDEV), 1)
    other = dev + 1 - 2 * gz
    other_c = pltpu.roll(c1, lax.rem(NDEV - other, NDEV), 1)

    def at_lane(c, index):
        return c[:, index % NDEV:index % NDEV + 1]

    def spread(vectors, c):
        total = None
        for a, v in enumerate(vectors):
            term = v * c[a:a + 1, :]
            total = term if total is None else total + term
        return total

    mine, theirs = at_lane(own_c, 0), at_lane(other_c, 0)
    for z in range(CZ):
        pc_ref[z, :CX, :CY] = spread([b_ref[a, pl.ds(source_of(z, gz), 1)][0] for a in range(8)], mine)
    for j in range(2):
        pc_ref[CZ + j, :CX, :CY] = spread([q_in[10 + 2 * a + j] for a in range(8)], theirs)
    for z in range(10):
        pc_ref[z, CX:, :] = jnp.zeros((EX - CX, EY), jnp.float32)
    for step_x, ref, other in ((16, xh_ref, xhq_ref), (-16, xl_ref, xlq_ref)):
        for d in range(2):
            rows = spread([ref[16 * a + 8 * d:16 * a + 8 * d + 8, :] for a in range(8)], at_lane(own_c, step_x))
            to = CX + d if step_x > 0 else EX - 1 - d
            for z in range(CZ):
                pc_ref[z, to:to + 1, :CY] = rows[z:z + 1]
        to = CX if step_x > 0 else EX - 1
        last = other[LAST_ROW - FIELD_ROW:LAST_ROW - FIELD_ROW + 8, :] * at_lane(other_c, step_x)
        pc_ref[CZ, to:to + 1, :CY] = jnp.sum(last, axis=0, keepdims=True)

    lane16 = lax.broadcasted_iota(jnp.int32, (CX, 128), 1)
    lane8 = lax.broadcasted_iota(jnp.int32, (8, 128), 1)

    def by_group(index, c, lane):
        total = jnp.zeros(lane.shape, jnp.float32)
        for a in range(8):
            total = jnp.where(index == a, c[a:a + 1, :], total)
        return total

    def columns(ref, c):
        v = ref[...][:CX, 128:] * by_group(lane16 // 16, c, lane16)
        for shift in (64, 32, 16):
            v = v + pltpu.roll(v, shift, 1)
        return v

    def place_columns(z, high, low, layer):
        pc_ref[z, :CX, CY:] = jnp.where(lane16 < 2, pltpu.roll(high, (-2 * layer) % 128, 1), jnp.where(
            lane16 >= 126, pltpu.roll(low, (126 - 2 * layer) % 128, 1), 0.0))

    high, low = columns(yh_ref, at_lane(own_c, 2)), columns(yl_ref, at_lane(own_c, -2))
    for z in range(CZ):
        place_columns(z, high, low, z)
    high, low = columns(yhq_ref, at_lane(other_c, 2)), columns(ylq_ref, at_lane(other_c, -2))
    for j in range(2):
        place_columns(CZ + j, high, low, CZ - 1 - j)

    def corner(ref, side, c):
        v = ref[...][CX:, 128 * side:128 * side + 128] * by_group((lane8 - CORNER_LANE) // 4, c, lane8)
        v = jnp.where((lane8 >= CORNER_LANE) & (lane8 < CORNER_LANE + 32), v, 0.0)
        for shift in (112, 120, 124):
            v = v + pltpu.roll(v, shift, 1)
        return v

    for side, step_x in enumerate((16, -16)):
        high = corner(yh_ref, side, at_lane(own_c, step_x + 2))
        low = corner(yl_ref, side, at_lane(own_c, step_x - 2))
        rows = jnp.where(lane8 < 4, pltpu.roll(high, 128 - CORNER_LANE, 1), jnp.where(
            lane8 >= 124, pltpu.roll(low, 124 - CORNER_LANE, 1), 0.0))
        to = EX - 1 if side else CX
        for z in range(CZ):
            pc_ref[z, to:to + 1, CY:] = rows[z:z + 1]

    def at(z, ref):
        return apply_at(z, ref[z], ref[z + 1], ref[z - 1] if z else None, dg_ref[z], wx_ref[z],
                        wy_ref[z], wz_ref[z], wz_ref[z - 1] if z else None)

    def out_z(z):
        return z + gz * (CZ - 1 - 2 * z)

    def keep(ref, z, value):
        ref[pl.ds(out_z(z), 1)] = value[None, :CX, :CY]

    for z in range(9):
        image = u_ref[z] + at(z, pc_ref)
        residual = r_ref[z] - step * image
        q_ref[z] = iv_ref[z] * residual
        if z < CZ:
            keep(res_ref, z, residual)
            pre = s_ref[z, :CX, :CY] + pc_ref[z, :CX, :CY]
            keep(pre_ref, z, pre)
            keep(sol_ref, z, step * pre)
    own_c2 = pltpu.roll(c2, lax.rem(NDEV - dev, NDEV), 1)
    partial = jnp.zeros((8, 128), jnp.float32)
    for z in range(CZ):
        residual = res_ref[pl.ds(out_z(z), 1)][0]
        second = q_ref[z, :CX, :CY] + iv_ref[z, :CX, :CY] * (residual - at(z, q_ref)[:CX, :CY])
        partial = partial + fold(residual * second)
        for b in range(8):
            second = second + b_ref[b, pl.ds(out_z(z), 1)][0] * own_c2[b:b + 1, 0:1]
        keep(refined_ref, z, second)
    part_ref[...] = jnp.sum(partial, axis=0, keepdims=True)
    spot = lax.broadcasted_iota(jnp.int32, (1, 128), 1)
    scal_ref[...] = jnp.where(spot == 0, g2c2, rz)


def finish_kernel(parts_ref, scal_ref, refined_ref, pre_ref, out_ref):
    growth = (total_of(parts_ref[...]) + scal_ref[:, 0:1]) / scal_ref[:, 1:2]
    for z in range(CZ):
        out_ref[z] = refined_ref[z] + growth * pre_ref[z]


def call(kernel, out_shapes, scratch, n_args, smem_first=False):
    whole = pl.BlockSpec(memory_space=pltpu.VMEM)
    specs = [whole] * n_args
    if smem_first:
        specs[0] = pl.BlockSpec(memory_space=pltpu.SMEM)
    return pl.pallas_call(
        kernel,
        out_shape=[jax.ShapeDtypeStruct(s, jnp.float32) for s in out_shapes],
        in_specs=specs,
        out_specs=[whole] * len(out_shapes),
        scratch_shapes=[pltpu.VMEM(s, jnp.float32) for s in scratch],
        compiler_params=pltpu.CompilerParams(vmem_limit_bytes=VMEM_LIMIT),
    )


def ring(axis, to):
    n = lax.axis_size(axis)
    return [(i, (i + to) % n) for i in range(n)]


def gather_rows(row):
    rows = jnp.broadcast_to(row[None], (NDEV,) + row.shape)
    return lax.all_to_all(rows, AXES, 0, 0, tiled=False)


def local(right_side, conductivity, storage, basis):
    pos = jnp.stack([lax.axis_index(a) for a in AXES]).astype(jnp.int32)
    swap = [(0, 1), (1, 0)]

    def exchange(axis, hi, lo):
        return lax.ppermute(lo, axis, ring(axis, -1)), lax.ppermute(hi, axis, ring(axis, 1))

    box, faces, small = (CZ, CX, CY), (FACE_ROWS, CY), (8, 256)
    fields = jnp.stack([conductivity, storage, right_side])
    b = basis.astype(jnp.float32)
    hi, lo, small_hi, small_lo, layers = call(
        pack_x_kernel, [faces, faces, small, small, (26, CX, CY)], [], 3, True)(pos, fields, b)
    corner_high, corner_low = exchange("gx", small_hi, small_lo)
    main_hi, main_lo = call(pack_y_kernel, [(CX, 256)] * 2, [], 3, True)(pos, fields, b)

    def with_corners(main, half):
        columns = slice(128 * half, 128 * half + 128)
        return jnp.concatenate(
            [main, jnp.concatenate([corner_high[:, columns], corner_low[:, columns]], axis=1)], axis=0)

    y_hi, y_lo = with_corners(main_hi, 1), with_corners(main_lo, 0)
    y_hi, y_lo, hi, lo, layers, gate = lax.optimization_barrier((y_hi, y_lo, hi, lo, layers, pos))
    y_high, y_low = exchange("gy", y_hi, y_lo)
    x_high, x_low = exchange("gx", hi, lo)
    other_layers = lax.ppermute(layers, "gz", swap)
    part, = call(gram_kernel, [(44 * 8, 128)], [], 3, True)(gate, fields, b)
    y_high, y_low, x_high, x_low, other_layers, part = lax.optimization_barrier(
        (y_high, y_low, x_high, x_low, other_layers, part))
    other_yh = lax.ppermute(y_high, "gz", swap)
    other_yl = lax.ppermute(y_low, "gz", swap)
    other_xh = lax.ppermute(x_high[FIELD_ROW:], "gz", swap)
    other_xl = lax.ppermute(x_low[FIELD_ROW:], "gz", swap)

    ext = (EZ, EX, EY)
    pay, r_ext, wx, wy, wz, dg, iv, s, u = call(
        prepare_kernel, [(2, 128)] + [ext] * 8, [ext, ext, ext, (2048, 128)], 17, True,
    )(pos, fields, part, b, other_layers, hi, lo, x_high, x_low, other_xh, other_xl,
      y_hi, y_lo, y_high, y_low, other_yh, other_yl)
    gathered = gather_rows(pay).reshape(NDEV, 256)
    sol, res, pre, refined, total, scal = call(
        coarse_kernel, [box] * 4 + [(1, 128)] * 2,
        [(2, 256, 128), (384, 256), ext, ext], 20, True,
    )(pos, gathered, r_ext, b, other_layers, x_high, x_low, other_xh, other_xl,
      y_high, y_low, other_yh, other_yl, wx, wy, wz, dg, iv, s, u)
    parts = gather_rows(total).reshape(NDEV, 128)
    direction, = call(finish_kernel, [box], [], 4)(parts, scal, refined, pre)
    return sol, res, direction


def solution(mesh):
    spec = P("gz", "gx", "gy")
    return jax.shard_map(
        local,
        mesh=mesh,
        in_specs=(spec, spec, spec, P(None, "gz", "gx", "gy")),
        out_specs=(spec, spec, spec),
        check_vma=False,
    )
```

```python
import functools

import jax
import jax.numpy as jnp
from jax import lax
from jax.experimental import pallas as pl
from jax.experimental.pallas import tpu as pltpu
from jax.sharding import PartitionSpec as P

KITERS = 6
RELAXATION = 0.6
HIGHEST = lax.Precision.HIGHEST
AXES = ("gx", "gy", "gz")
CZ, CX, CY = 8, 16, 256
EZ, EX, EY = 12, 24, 384
NDEV = 256
PAIRS = [(a, b) for a in range(8) for b in range(a, 8)]
ROW_Z, ROW_Y, ROW_X, ROW_OWN, ROW_RS, ROW_SAS, ROW_G, ROW_H = 0, 64, 128, 192, 228, 229, 232, 240
DEPTHS = (4, 3, 3)
STEPS = [(f, d) for f in range(3) for d in range(DEPTHS[f])]
FIELD_ROW, LAST_ROW, CORNER_ROW = 128, 208, 216
FACE_LANE = 96
VMEM_LIMIT = 24 * 1024 * 1024


def harmonic(k, other):
    return 2.0 * k * other / jnp.maximum(k + other, 1e-30)


def y_next(v):
    return pltpu.roll(v, v.shape[1] - 1, 1)


def y_prev(v):
    return pltpu.roll(v, 1, 1)


def x_next(v):
    return pltpu.roll(v, v.shape[0] - 1, 0)


def x_prev(v):
    return pltpu.roll(v, 1, 0)


def apply_at(z, v, v_up, v_down, diag, wx, wy, wz_up, wz_down):
    total = diag * v - wy * y_next(v) - y_prev(wy * v) - wx * x_next(v) - x_prev(wx * v)
    if v_up is not None:
        total = total - wz_up * v_up
    if v_down is not None:
        total = total - wz_down * v_down
    return total


def fold(v):
    return (v[:8, :128] + v[8:, :128]) + (v[:8, 128:] + v[8:, 128:])


def flag(inside):
    return jnp.where(inside, 1.0, 0.0).astype(jnp.float32)


def source_of(z, gz):
    return z + gz * (CZ - 1 - 2 * z)


def pack_x_kernel(pos_ref, f_ref, b_ref, hi_ref, lo_ref, q_ref):
    gz = pos_ref[2]
    for z in range(CZ):
        src, j = source_of(z, gz), CZ - 1 - z
        fields = [f_ref[f, pl.ds(src, 1)][0] for f in range(3)]
        for t, (f, d) in enumerate(STEPS):
            row = FIELD_ROW + 8 * t + z
            hi_ref[row:row + 1, :] = fields[f][CX - 1 - d:CX - d]
            lo_ref[row:row + 1, :] = fields[f][d:d + 1]
        if j < 4:
            q_ref[j] = fields[0]
        if j < 3:
            q_ref[4 + j] = fields[1]
            q_ref[7 + j] = fields[2]
        for a in range(8):
            v = b_ref[a, pl.ds(src, 1)][0]
            for d in range(2):
                row = 16 * a + 8 * d + z
                hi_ref[row:row + 1, :] = v[CX - 1 - d:CX - d]
                lo_ref[row:row + 1, :] = v[d:d + 1]
            if j == 0:
                hi_ref[LAST_ROW + a:LAST_ROW + a + 1, :] = v[CX - 1:CX]
                lo_ref[LAST_ROW + a:LAST_ROW + a + 1, :] = v[0:1]
            if j < 2:
                q_ref[10 + 2 * a + j] = v


def pack_y_kernel(pos_ref, f_ref, b_ref, hi_ref, lo_ref):
    gz = pos_ref[2]
    lane = lax.broadcasted_iota(jnp.int32, (CX, 128), 1)
    hi = [jnp.zeros((CX, 128), jnp.float32)] * 2
    lo = [jnp.zeros((CX, 128), jnp.float32)] * 2

    def put(half, v, width, offset):
        mask = (lane >= offset) & (lane < offset + width)
        hi[half] = jnp.where(mask, pltpu.roll(v[:, 128:], (offset + width) % 128, 1), hi[half])
        lo[half] = jnp.where(mask, pltpu.roll(v[:, :128], offset, 1), lo[half])

    for z in range(CZ):
        src = source_of(z, gz)
        for f in range(3):
            v = f_ref[f, pl.ds(src, 1)][0]
            put(0, v, 4, 32 * f + 4 * z)
            if f == 0:
                put(0, v, 1, FACE_LANE + 2 * z + 1)
        for a in range(8):
            put(1, b_ref[a, pl.ds(src, 1)][0], 2, 16 * a + 2 * z)
    for half in range(2):
        hi_ref[:, 128 * half:128 * half + 128] = hi[half]
        lo_ref[:, 128 * half:128 * half + 128] = lo[half]


def gram_kernel(pos_ref, f_ref, b_ref, part_ref):
    gz = pos_ref[2]
    part_ref[...] = jnp.zeros_like(part_ref)
    rows = lax.broadcasted_iota(jnp.int32, (CX, CY), 0)
    lanes = lax.broadcasted_iota(jnp.int32, (CX, CY), 1)

    def add(row, value):
        part_ref[8 * row:8 * row + 8, :] += value

    def body(z, carry):
        src, up, down = source_of(z, gz), jnp.minimum(z + 1, CZ - 1), jnp.maximum(z - 1, 0)
        k, st, r = (f_ref[f, pl.ds(src, 1)][0] for f in range(3))
        src_up, src_down = source_of(up, gz), source_of(down, gz)
        wy = jnp.where(lanes == CY - 1, 0.0, harmonic(k, y_next(k)))
        wx = jnp.where(rows == CX - 1, 0.0, harmonic(k, x_next(k)))
        wz_up = jnp.where(z < CZ - 1, harmonic(k, f_ref[0, pl.ds(src_up, 1)][0]), 0.0)
        wz_down = jnp.where(z > 0, harmonic(k, f_ref[0, pl.ds(src_down, 1)][0]), 0.0)
        diag = st + wy + y_prev(wy) + wx + x_prev(wx) + wz_up + wz_down
        basis = [b_ref[a, pl.ds(src, 1)][0] for a in range(8)]
        for b in range(8):
            add(36 + b, fold(basis[b] * r))
            image = apply_at(z, basis[b], b_ref[b, pl.ds(src_up, 1)][0],
                             b_ref[b, pl.ds(src_down, 1)][0], diag,
                             wx, wy, wz_up, wz_down)
            for a in range(b + 1):
                add(PAIRS.index((a, b)), fold(basis[a] * image))
        return carry

    lax.fori_loop(0, CZ, body, 0)


def prepare_kernel(pos_ref, f_in, part_ref, b_ref, q_ref, hi_ref, lo_ref, xh_ref, xl_ref, xhq_ref,
                   xlq_ref, ys_hi_ref, ys_lo_ref, yh_ref, yl_ref, yhq_ref, ylq_ref,
                   pay_ref, r_ref, wx_ref, wy_ref, wz_ref, dg_ref, iv_ref, s_ref, u_ref,
                   k_ref, st_ref, first_ref, acc_ref):
    gx, gy, gz = pos_ref[0], pos_ref[1], pos_ref[2]
    x_high, x_low = flag(gx < 15), flag(gx > 0)
    y_high, y_low = flag(gy < 7), flag(gy > 0)
    lane16 = lax.broadcasted_iota(jnp.int32, (CX, 128), 1)
    lane8 = lax.broadcasted_iota(jnp.int32, (8, 128), 1)
    lane24 = lax.broadcasted_iota(jnp.int32, (EX, 128), 1)
    row24 = lax.broadcasted_iota(jnp.int32, (EX, 128), 0)
    inside_x = jnp.where(row24 < CX, 1.0, jnp.where(row24 < CX + 4, x_high, x_low))
    outs = (k_ref, st_ref, r_ref)

    def main(f, z, value, high, low, layer):
        ref, offset = outs[f], 32 * f + 4 * layer
        high = pltpu.roll(high[:, :128], -offset % 128, 1)
        low = pltpu.roll(low[:, :128], (124 - offset) % 128, 1)
        if f == 0:
            high, low = high * (inside_x * y_high), low * (inside_x * y_low)
        ref[z, :CX, :CY] = value
        ref[z, :, CY:] = jnp.where(lane24 < 4, high, jnp.where(lane24 >= 124, low, 1.0))
        if f:
            ref[z, CX:, :CY] = jnp.ones((EX - CX, CY), jnp.float32)

    def edges(t, sides, places):
        f, d = STEPS[t]
        for side, (ref, inside, row) in enumerate(sides):
            wide = ref[row + 8 * t:row + 8 * t + 8, :]
            if f == 0:
                wide = wide * inside
            to = EX - 1 - d if side else CX + d
            for z, layer in places:
                outs[f][z, to:to + 1, :CY] = wide[layer:layer + 1]

    high, low = yh_ref[...], yl_ref[...]
    for z in range(CZ):
        src = source_of(z, gz)
        for f in range(3):
            main(f, z, f_in[f, pl.ds(src, 1)][0], high, low, z)
    sides = ((xh_ref, x_high, FIELD_ROW), (xl_ref, x_low, FIELD_ROW))
    for t in range(len(STEPS)):
        edges(t, sides, [(z, z) for z in range(CZ)])
    high, low = yhq_ref[...], ylq_ref[...]
    first_layer = (0, 4, 7)
    for f in range(3):
        for j in range(DEPTHS[f]):
            main(f, CZ + j, q_ref[first_layer[f] + j], high, low, CZ - 1 - j)
    sides = ((xhq_ref, x_high, 0), (xlq_ref, x_low, 0))
    for t, (f, d) in enumerate(STEPS):
        edges(t, sides, [(CZ + j, CZ - 1 - j) for j in range(DEPTHS[f])])

    for z in range(11):
        k = k_ref[z]
        wy_ref[z] = harmonic(k, y_next(k))
        wx_ref[z] = harmonic(k, x_next(k))
        wz_ref[z] = harmonic(k, k_ref[z + 1])
    for z in range(11):
        wy, wx = wy_ref[z], wx_ref[z]
        diag = st_ref[z] + wy + y_prev(wy) + wx + x_prev(wx) + wz_ref[z]
        if z:
            diag = diag + wz_ref[z - 1]
        inverse = RELAXATION / jnp.maximum(diag, 1e-3)
        dg_ref[z] = diag
        iv_ref[z] = inverse
        first_ref[z] = inverse * r_ref[z]

    def at(z, ref):
        return apply_at(z, ref[z], ref[z + 1], ref[z - 1] if z else None, dg_ref[z], wx_ref[z],
                        wy_ref[z], wz_ref[z], wz_ref[z - 1] if z else None)

    for z in range(10):
        s_ref[z] = first_ref[z] + iv_ref[z] * (r_ref[z] - at(z, first_ref))
    for z in range(9):
        u_ref[z] = at(z, s_ref)

    def set_row(row, value):
        acc_ref[8 * row:8 * row + 8, :] = value

    def layers(products):
        total = None
        for z in range(CZ):
            total = products(z) if total is None else total + products(z)
        return fold(total)

    def own(ref, z):
        return ref[z, :CX, :CY]

    def basis(a, z):
        return b_ref[a, pl.ds(source_of(z, gz), 1)][0]

    acc_ref[8 * ROW_RS:8 * ROW_G, :] = jnp.zeros((8 * (ROW_G - ROW_RS), 128), jnp.float32)
    acc_ref[8 * (ROW_H + 8):2048, :] = jnp.zeros((2048 - 8 * (ROW_H + 8), 128), jnp.float32)
    set_row(ROW_RS, layers(lambda z: own(r_ref, z) * own(s_ref, z)))
    set_row(ROW_SAS, layers(lambda z: own(u_ref, z) * own(s_ref, z)))
    for a in range(8):
        set_row(ROW_H + a, layers(lambda z: basis(a, z) * own(u_ref, z)))
    acc_ref[8 * ROW_G:8 * (ROW_G + 8), :] = part_ref[8 * 36:8 * 44, :]

    odd = (lane16 < 16) & (lax.rem(lane16, 2) == 1)
    group = lane8 // 16

    def y_weight(own_ref, beside_ref, inside):
        weight = harmonic(own_ref[...][:CX, :128], beside_ref[...][:CX, :128] * inside)
        weight = jnp.where(odd, pltpu.roll(weight, 128 - FACE_LANE, 1), 0.0)
        for shift in (16, 32, 64):
            weight = weight + pltpu.roll(weight, shift, 1)
        return weight

    def turned(v, d):
        return pltpu.roll(v, 128 - 16 * d, 1) if d else v

    mine = ys_hi_ref[...][:CX, 128:]
    first_mine = pltpu.roll(ys_lo_ref[...][:CX, 128:], 1, 1)
    theirs = pltpu.roll(yh_ref[...][:CX, 128:], 1, 1)
    weighted = y_weight(ys_hi_ref, yh_ref, y_high) * mine
    first_weighted = y_weight(ys_lo_ref, yl_ref, y_low) * first_mine
    face_y = {}
    for d in range(8):
        product = -weighted * turned(theirs, d)
        product = product[:8] + product[8:]
        for a in range(8):
            set_row(ROW_Y + 8 * ((a + d) % 8) + a, jnp.where(group == a, product, 0.0))
        if d < 5:
            inner = weighted * turned(mine, d) + first_weighted * turned(first_mine, d)
            face_y[d] = inner[:8] + inner[8:]

    wz_face = own(wz_ref, CZ - 1)
    wx_face = harmonic(hi_ref[FIELD_ROW:FIELD_ROW + 8, :], xh_ref[FIELD_ROW:FIELD_ROW + 8, :] * x_high)
    wx_first = harmonic(lo_ref[FIELD_ROW:FIELD_ROW + 8, :], xl_ref[FIELD_ROW:FIELD_ROW + 8, :] * x_low)
    for a in range(8):
        za = wz_face * basis(a, CZ - 1)
        xa = wx_face * hi_ref[16 * a:16 * a + 8, :]
        xa_first = wx_first * lo_ref[16 * a:16 * a + 8, :]
        for b in range(8):
            row = 8 * b + a
            set_row(ROW_Z + row, -fold(za * q_ref[10 + 2 * b]))
            x = xa * xh_ref[16 * b:16 * b + 8, :]
            set_row(ROW_X + row, -(x[:, :128] + x[:, 128:]))
            if b < a:
                continue
            x = xa * hi_ref[16 * b:16 * b + 8, :] + xa_first * lo_ref[16 * b:16 * b + 8, :]
            pair = PAIRS.index((a, b))
            value = part_ref[8 * pair:8 * pair + 8, :] + fold(za * basis(b, CZ - 1)) + x[:, :128] + x[:, 128:]
            d, place = (b - a, a) if b - a < 5 else (a - b + 8, b)
            set_row(ROW_OWN + pair, value + jnp.where(group == place, face_y[d], 0.0))

    total = acc_ref[pl.ds(0, 256, stride=8), :]
    for sub in range(1, 8):
        total = total + acc_ref[pl.ds(sub, 256, stride=8), :]
    summed = lax.dot_general(jnp.ones((8, 128), jnp.float32), total, (((1,), (1,)), ((), ())),
                             precision=HIGHEST, preferred_element_type=jnp.float32)
    pay_ref[0:1, :] = summed[0:1, :128]
    pay_ref[1:2, :] = summed[0:1, 128:]


def total_of(v):
    v = jnp.sum(v, axis=0, keepdims=True)
    if v.shape[1] == 256:
        v = v[:, :128] + v[:, 128:]
    return jnp.sum(v, axis=1, keepdims=True)


def dot(left, right):
    v = left * right
    return total_of(v[:, :128] + v[:, 128:])


def coarse_solve(tile_ref, lane_even):
    def partner(c):
        return jnp.where(lane_even, pltpu.roll(c, NDEV - 1, 1), pltpu.roll(c, 1, 1))

    def apply_e(c):
        shifted = [c, partner(c), pltpu.roll(c, NDEV - 2, 1), pltpu.roll(c, NDEV - 16, 1),
                   pltpu.roll(c, 2, 1), pltpu.roll(c, 16, 1)]
        total = None
        for o, v in enumerate(shifted):
            part = None
            for b in range(8):
                tile = (tile_ref[8 * (8 * o + b):8 * (8 * o + b) + 8, :])
                term = tile * v[b:b + 1, :]
                part = term if part is None else part + term
            total = part if total is None else total + part
        return total

    def solve(g):
        remainder, search, image = g, g, apply_e(g)
        current, along = dot(g, g), dot(g, image)
        solution = jnp.zeros_like(g)
        for iteration in range(KITERS):
            step = current / along
            solution = solution + step * search
            remainder = remainder - step * image
            if iteration == KITERS - 1:
                break
            applied = apply_e(remainder)
            updated = dot(remainder, remainder)
            ratio = updated / current
            along = dot(remainder, applied) + ratio * (2.0 * dot(remainder, image) + ratio * along)
            search = remainder + ratio * search
            image = applied + ratio * image
            current = updated
        return solution, g - remainder

    return solve


def coarse_kernel(pos_ref, gath_ref, r_ref, b_ref, q_in, xh_ref, xl_ref, xhq_ref, xlq_ref,
                  yh_ref, yl_ref, yhq_ref, ylq_ref, wx_ref, wy_ref, wz_ref, dg_ref, iv_ref, s_ref, u_ref,
                  sol_ref, res_ref, pre_ref, refined_ref, part_ref, scal_ref,
                  t_ref, tile_ref, pc_ref, q_ref):
    gz = pos_ref[2]
    dev = (pos_ref[0] * 8 + pos_ref[1]) * 2 + gz
    turned = gath_ref[...].T
    t_ref[0] = turned[:, :128]
    t_ref[1] = turned[:, 128:]

    def rows_at(index):
        return jnp.concatenate([t_ref[0, index, :], t_ref[1, index, :]], axis=1)

    for b in range(8):
        for a in range(8):
            row = ROW_OWN + PAIRS.index((min(a, b), max(a, b)))
            tile_ref[8 * b + a:8 * b + a + 1, :] = turned[row:row + 1, :]
    tile_ref[64:256, :] = turned[0:192, :]
    for b in range(8):
        tile_ref[256 + 8 * b:264 + 8 * b, :] = pltpu.roll(rows_at(pl.ds(ROW_Y + b, 8, stride=8)), 2, 1)
        tile_ref[320 + 8 * b:328 + 8 * b, :] = pltpu.roll(rows_at(pl.ds(ROW_X + b, 8, stride=8)), 16, 1)
    lane = lax.broadcasted_iota(jnp.int32, (8, NDEV), 1)
    solve = coarse_solve(tile_ref, lax.rem(lane, 2) == 0)
    g = turned[ROW_G:ROW_G + 8]
    h = turned[ROW_H:ROW_H + 8]
    rs = turned[ROW_RS:ROW_RS + 1]
    sas = turned[ROW_SAS:ROW_SAS + 1]
    c1, ec1 = solve(g)
    rz = total_of(rs) + dot(g, c1)
    curvature = total_of(sas) + dot(2.0 * h + ec1, c1)
    step = rz / curvature
    g2 = g - step * (h + ec1)
    c2, _ = solve(g2)
    g2c2 = dot(g2, c2)

    own_c = pltpu.roll(c1, lax.rem(NDEV - dev, NDEV), 1)
    other = dev + 1 - 2 * gz
    other_c = pltpu.roll(c1, lax.rem(NDEV - other, NDEV), 1)

    def at_lane(c, index):
        return c[:, index % NDEV:index % NDEV + 1]

    def spread(vectors, c):
        total = None
        for a, v in enumerate(vectors):
            term = v * c[a:a + 1, :]
            total = term if total is None else total + term
        return total

    mine, theirs = at_lane(own_c, 0), at_lane(other_c, 0)
    for z in range(CZ):
        pc_ref[z, :CX, :CY] = spread([b_ref[a, pl.ds(source_of(z, gz), 1)][0] for a in range(8)], mine)
    for j in range(2):
        pc_ref[CZ + j, :CX, :CY] = spread([q_in[10 + 2 * a + j] for a in range(8)], theirs)
    for z in range(10):
        pc_ref[z, CX:, :CY] = jnp.zeros((EX - CX, CY), jnp.float32)
    for step_x, ref, other in ((16, xh_ref, xhq_ref), (-16, xl_ref, xlq_ref)):
        for d in range(2):
            rows = spread([ref[16 * a + 8 * d:16 * a + 8 * d + 8, :] for a in range(8)], at_lane(own_c, step_x))
            to = CX + d if step_x > 0 else EX - 1 - d
            for z in range(CZ):
                pc_ref[z, to:to + 1, :CY] = rows[z:z + 1]
        to = CX if step_x > 0 else EX - 1
        last = other[LAST_ROW - FIELD_ROW:LAST_ROW - FIELD_ROW + 8, :] * at_lane(other_c, step_x)
        pc_ref[CZ, to:to + 1, :CY] = jnp.sum(last, axis=0, keepdims=True)

    lane24 = lax.broadcasted_iota(jnp.int32, (EX, 128), 1)
    row24 = lax.broadcasted_iota(jnp.int32, (EX, 128), 0)

    def by_group(c):
        total = jnp.zeros((EX, 128), jnp.float32)
        for a in range(8):
            total = jnp.where(lane24 // 16 == a, c[a:a + 1, :], total)
        return total

    def columns(ref, c, step_y, corners):
        high_x = low_x = 0.0
        if corners:
            high_x, low_x = by_group(at_lane(c, 16 + step_y)), by_group(at_lane(c, step_y - 16))
        v = jnp.where(row24 < CX, by_group(at_lane(c, step_y)), jnp.where(row24 < CX + 4, high_x, low_x))
        v = v * ref[...][:, 128:]
        for shift in (64, 32, 16):
            v = v + pltpu.roll(v, shift, 1)
        return v

    def place_columns(z, high, low, layer):
        pc_ref[z, :, CY:] = jnp.where(lane24 < 2, pltpu.roll(high, (-2 * layer) % 128, 1), jnp.where(
            lane24 >= 126, pltpu.roll(low, (126 - 2 * layer) % 128, 1), 0.0))

    high, low = columns(yh_ref, own_c, 2, True), columns(yl_ref, own_c, -2, True)
    for z in range(CZ):
        place_columns(z, high, low, z)
    high, low = columns(yhq_ref, other_c, 2, False), columns(ylq_ref, other_c, -2, False)
    for j in range(2):
        place_columns(CZ + j, high, low, CZ - 1 - j)

    def at(z, ref):
        return apply_at(z, ref[z], ref[z + 1], ref[z - 1] if z else None, dg_ref[z], wx_ref[z],
                        wy_ref[z], wz_ref[z], wz_ref[z - 1] if z else None)

    def out_z(z):
        return z + gz * (CZ - 1 - 2 * z)

    def keep(ref, z, value):
        ref[pl.ds(out_z(z), 1)] = value[None, :CX, :CY]

    for z in range(9):
        image = u_ref[z] + at(z, pc_ref)
        residual = r_ref[z] - step * image
        q_ref[z] = iv_ref[z] * residual
        if z < CZ:
            keep(res_ref, z, residual)
            pre = s_ref[z, :CX, :CY] + pc_ref[z, :CX, :CY]
            keep(pre_ref, z, pre)
            keep(sol_ref, z, step * pre)
    own_c2 = pltpu.roll(c2, lax.rem(NDEV - dev, NDEV), 1)
    partial = jnp.zeros((8, 128), jnp.float32)
    for z in range(CZ):
        residual = res_ref[pl.ds(out_z(z), 1)][0]
        second = q_ref[z, :CX, :CY] + iv_ref[z, :CX, :CY] * (residual - at(z, q_ref)[:CX, :CY])
        partial = partial + fold(residual * second)
        for b in range(8):
            second = second + b_ref[b, pl.ds(out_z(z), 1)][0] * own_c2[b:b + 1, 0:1]
        keep(refined_ref, z, second)
    part_ref[...] = jnp.sum(partial, axis=0, keepdims=True)
    spot = lax.broadcasted_iota(jnp.int32, (1, 128), 1)
    scal_ref[...] = jnp.where(spot == 0, g2c2, rz)


def finish_kernel(parts_ref, scal_ref, refined_ref, pre_ref, out_ref):
    growth = (total_of(parts_ref[...]) + scal_ref[:, 0:1]) / scal_ref[:, 1:2]
    for z in range(CZ):
        out_ref[z] = refined_ref[z] + growth * pre_ref[z]


def call(kernel, out_shapes, scratch, n_args, smem_first=False):
    whole = pl.BlockSpec(memory_space=pltpu.VMEM)
    specs = [whole] * n_args
    if smem_first:
        specs[0] = pl.BlockSpec(memory_space=pltpu.SMEM)
    return pl.pallas_call(
        kernel,
        out_shape=[jax.ShapeDtypeStruct(s, jnp.float32) for s in out_shapes],
        in_specs=specs,
        out_specs=[whole] * len(out_shapes),
        scratch_shapes=[pltpu.VMEM(s, jnp.float32) for s in scratch],
        compiler_params=pltpu.CompilerParams(vmem_limit_bytes=VMEM_LIMIT),
    )


def ring(axis, to):
    n = lax.axis_size(axis)
    return [(i, (i + to) % n) for i in range(n)]


def gather_rows(row):
    rows = jnp.broadcast_to(row[None], (NDEV,) + row.shape)
    return lax.all_to_all(rows, AXES, 0, 0, tiled=False)


def local(right_side, conductivity, storage, basis):
    pos = jnp.stack([lax.axis_index(a) for a in AXES]).astype(jnp.int32)
    swap = [(0, 1), (1, 0)]

    def exchange(axis, hi, lo):
        return lax.ppermute(lo, axis, ring(axis, -1)), lax.ppermute(hi, axis, ring(axis, 1))

    box, faces = (CZ, CX, CY), (CORNER_ROW, CY)
    fields = jnp.stack([conductivity, storage, right_side])
    b = basis.astype(jnp.float32)
    main_hi, main_lo = call(pack_y_kernel, [(CX, 256)] * 2, [], 3, True)(pos, fields, b)
    main_high, main_low = exchange("gy", main_hi, main_lo)
    hi, lo, layers = call(pack_x_kernel, [faces, faces, (26, CX, CY)], [], 3, True)(pos, fields, b)
    other_layers = lax.ppermute(layers, "gz", swap)
    hi = jnp.concatenate([hi, main_high[CX - 4:], main_low[CX - 4:]], axis=0)
    lo = jnp.concatenate([lo, main_high[:4], main_low[:4]], axis=0)
    hi, lo, main_high, main_low, gate = lax.optimization_barrier((hi, lo, main_high, main_low, pos))
    x_high, x_low = exchange("gx", hi, lo)
    other_main = lax.ppermute(jnp.concatenate([main_high, main_low], axis=0), "gz", swap)
    part, = call(gram_kernel, [(44 * 8, 128)], [], 3, True)(gate, fields, b)
    x_high, x_low, other_layers, other_main, part = lax.optimization_barrier(
        (x_high, x_low, other_layers, other_main, part))
    other_xh = lax.ppermute(x_high[FIELD_ROW:], "gz", swap)
    other_xl = lax.ppermute(x_low[FIELD_ROW:], "gz", swap)

    def with_corners(main, high, low, row):
        return jnp.concatenate([main, high[row:row + 4], low[row:row + 4]], axis=0)

    y_high = with_corners(main_high, x_high, x_low, CORNER_ROW)
    y_low = with_corners(main_low, x_high, x_low, CORNER_ROW + 4)
    other_yh = with_corners(other_main[:CX], other_xh, other_xl, CORNER_ROW - FIELD_ROW)
    other_yl = with_corners(other_main[CX:], other_xh, other_xl, CORNER_ROW - FIELD_ROW + 4)

    ext = (EZ, EX, EY)
    pay, r_ext, wx, wy, wz, dg, iv, s, u = call(
        prepare_kernel, [(2, 128)] + [ext] * 8, [ext, ext, ext, (2048, 128)], 17, True,
    )(pos, fields, part, b, other_layers, hi, lo, x_high, x_low, other_xh, other_xl,
      main_hi, main_lo, y_high, y_low, other_yh, other_yl)
    gathered = gather_rows(pay).reshape(NDEV, 256)
    sol, res, pre, refined, total, scal = call(
        coarse_kernel, [box] * 4 + [(1, 128)] * 2,
        [(2, 256, 128), (384, 256), ext, ext], 20, True,
    )(pos, gathered, r_ext, b, other_layers, x_high, x_low, other_xh, other_xl,
      y_high, y_low, other_yh, other_yl, wx, wy, wz, dg, iv, s, u)
    parts = gather_rows(total).reshape(NDEV, 128)
    direction, = call(finish_kernel, [box], [], 4)(parts, scal, refined, pre)
    return sol, res, direction


def solution(mesh):
    spec = P("gz", "gx", "gy")
    return jax.shard_map(
        local,
        mesh=mesh,
        in_specs=(spec, spec, spec, P(None, "gz", "gx", "gy")),
        out_specs=(spec, spec, spec),
        check_vma=False,
    )
```

```python
import functools

import jax
import jax.numpy as jnp
from jax import lax
from jax.experimental import pallas as pl
from jax.experimental.pallas import tpu as pltpu
from jax.sharding import PartitionSpec as P

KITERS = 6
RELAXATION = 0.6
HIGHEST = lax.Precision.HIGHEST
AXES = ("gx", "gy", "gz")
CZ, CX, CY = 8, 16, 256
EZ, EX, EY = 12, 24, 384
NDEV = 256
PAIRS = [(a, b) for a in range(8) for b in range(a, 8)]
ROW_Z, ROW_Y, ROW_X, ROW_OWN, ROW_RS, ROW_SAS, ROW_G, ROW_H = 0, 64, 128, 192, 228, 229, 232, 240
DEPTHS = (4, 3, 3)
STEPS = [(f, d) for f in range(3) for d in range(DEPTHS[f])]
FIELD_ROW, LAST_ROW, CORNER_ROW = 128, 208, 216
FACE_LANE = 96
VMEM_LIMIT = 24 * 1024 * 1024


def harmonic(k, other):
    return 2.0 * k * other / jnp.maximum(k + other, 1e-30)


def y_next(v):
    return pltpu.roll(v, v.shape[1] - 1, 1)


def y_prev(v):
    return pltpu.roll(v, 1, 1)


def x_next(v):
    return pltpu.roll(v, v.shape[0] - 1, 0)


def x_prev(v):
    return pltpu.roll(v, 1, 0)


def apply_at(z, v, v_up, v_down, diag, wx, wy, wz_up, wz_down):
    total = diag * v - wy * y_next(v) - y_prev(wy * v) - wx * x_next(v) - x_prev(wx * v)
    if v_up is not None:
        total = total - wz_up * v_up
    if v_down is not None:
        total = total - wz_down * v_down
    return total


def fold(v):
    return (v[:8, :128] + v[8:, :128]) + (v[:8, 128:] + v[8:, 128:])


def flag(inside):
    return jnp.where(inside, 1.0, 0.0).astype(jnp.float32)


def source_of(z, gz):
    return z + gz * (CZ - 1 - 2 * z)


def pack_x_kernel(pos_ref, f_ref, b_ref, hi_ref, lo_ref, q_ref):
    gz = pos_ref[2]
    for z in range(CZ):
        src, j = source_of(z, gz), CZ - 1 - z
        fields = [f_ref[f, pl.ds(src, 1)][0] for f in range(3)]
        for t, (f, d) in enumerate(STEPS):
            row = FIELD_ROW + 8 * t + z
            hi_ref[row:row + 1, :] = fields[f][CX - 1 - d:CX - d]
            lo_ref[row:row + 1, :] = fields[f][d:d + 1]
        if j < 4:
            q_ref[j] = fields[0]
        if j < 3:
            q_ref[4 + j] = fields[1]
            q_ref[7 + j] = fields[2]
        for a in range(8):
            v = b_ref[a, pl.ds(src, 1)][0]
            for d in range(2):
                row = 16 * a + 8 * d + z
                hi_ref[row:row + 1, :] = v[CX - 1 - d:CX - d]
                lo_ref[row:row + 1, :] = v[d:d + 1]
            if j == 0:
                hi_ref[LAST_ROW + a:LAST_ROW + a + 1, :] = v[CX - 1:CX]
                lo_ref[LAST_ROW + a:LAST_ROW + a + 1, :] = v[0:1]
            if j < 2:
                q_ref[10 + 2 * a + j] = v


def pack_y_kernel(pos_ref, f_ref, b_ref, hi_ref, lo_ref):
    gz = pos_ref[2]
    lane = lax.broadcasted_iota(jnp.int32, (CX, 128), 1)
    hi = [jnp.zeros((CX, 128), jnp.float32)] * 2
    lo = [jnp.zeros((CX, 128), jnp.float32)] * 2

    def put(half, v, width, offset):
        mask = (lane >= offset) & (lane < offset + width)
        hi[half] = jnp.where(mask, pltpu.roll(v[:, 128:], (offset + width) % 128, 1), hi[half])
        lo[half] = jnp.where(mask, pltpu.roll(v[:, :128], offset, 1), lo[half])

    for z in range(CZ):
        src = source_of(z, gz)
        for f in range(3):
            v = f_ref[f, pl.ds(src, 1)][0]
            put(0, v, 4, 32 * f + 4 * z)
            if f == 0:
                put(0, v, 1, FACE_LANE + 2 * z + 1)
        for a in range(8):
            put(1, b_ref[a, pl.ds(src, 1)][0], 2, 16 * a + 2 * z)
    for half in range(2):
        hi_ref[:, 128 * half:128 * half + 128] = hi[half]
        lo_ref[:, 128 * half:128 * half + 128] = lo[half]


def gram_kernel(pos_ref, f_ref, b_ref, part_ref):
    gz = pos_ref[2]
    part_ref[...] = jnp.zeros_like(part_ref)
    rows = lax.broadcasted_iota(jnp.int32, (CX, CY), 0)
    lanes = lax.broadcasted_iota(jnp.int32, (CX, CY), 1)

    def add(row, value):
        part_ref[8 * row:8 * row + 8, :] += value

    def body(z, carry):
        src, up, down = source_of(z, gz), jnp.minimum(z + 1, CZ - 1), jnp.maximum(z - 1, 0)
        k, st, r = (f_ref[f, pl.ds(src, 1)][0] for f in range(3))
        src_up, src_down = source_of(up, gz), source_of(down, gz)
        wy = jnp.where(lanes == CY - 1, 0.0, harmonic(k, y_next(k)))
        wx = jnp.where(rows == CX - 1, 0.0, harmonic(k, x_next(k)))
        wz_up = jnp.where(z < CZ - 1, harmonic(k, f_ref[0, pl.ds(src_up, 1)][0]), 0.0)
        wz_down = jnp.where(z > 0, harmonic(k, f_ref[0, pl.ds(src_down, 1)][0]), 0.0)
        diag = st + wy + y_prev(wy) + wx + x_prev(wx) + wz_up + wz_down
        basis = [b_ref[a, pl.ds(src, 1)][0] for a in range(8)]
        for b in range(8):
            add(36 + b, fold(basis[b] * r))
            image = apply_at(z, basis[b], b_ref[b, pl.ds(src_up, 1)][0],
                             b_ref[b, pl.ds(src_down, 1)][0], diag,
                             wx, wy, wz_up, wz_down)
            for a in range(b + 1):
                add(PAIRS.index((a, b)), fold(basis[a] * image))
        return carry

    lax.fori_loop(0, CZ, body, 0)


def prepare_kernel(pos_ref, f_in, part_ref, b_ref, q_ref, hi_ref, lo_ref, xh_ref, xl_ref, xhq_ref,
                   xlq_ref, ys_hi_ref, ys_lo_ref, yh_ref, yl_ref, yhq_ref, ylq_ref,
                   pay_ref, r_ref, wx_ref, wy_ref, wz_ref, dg_ref, iv_ref, s_ref, u_ref,
                   k_ref, st_ref, first_ref, acc_ref):
    gx, gy, gz = pos_ref[0], pos_ref[1], pos_ref[2]
    x_high, x_low = flag(gx < 15), flag(gx > 0)
    y_high, y_low = flag(gy < 7), flag(gy > 0)
    lane16 = lax.broadcasted_iota(jnp.int32, (CX, 128), 1)
    lane8 = lax.broadcasted_iota(jnp.int32, (8, 128), 1)
    lane24 = lax.broadcasted_iota(jnp.int32, (EX, 128), 1)
    row24 = lax.broadcasted_iota(jnp.int32, (EX, 128), 0)
    inside_x = jnp.where(row24 < CX, 1.0, jnp.where(row24 < CX + 4, x_high, x_low))
    outs = (k_ref, st_ref, r_ref)

    def main(f, z, value, high, low, layer):
        ref, offset = outs[f], 32 * f + 4 * layer
        high = pltpu.roll(high[:, :128], -offset % 128, 1)
        low = pltpu.roll(low[:, :128], (124 - offset) % 128, 1)
        if f == 0:
            high, low = high * (inside_x * y_high), low * (inside_x * y_low)
        ref[z, :CX, :CY] = value
        ref[z, :, CY:] = jnp.where(lane24 < 4, high, jnp.where(lane24 >= 124, low, 1.0))
        if f:
            ref[z, CX:, :CY] = jnp.ones((EX - CX, CY), jnp.float32)

    def edges(t, sides, places):
        f, d = STEPS[t]
        for side, (ref, inside, row) in enumerate(sides):
            wide = ref[row + 8 * t:row + 8 * t + 8, :]
            if f == 0:
                wide = wide * inside
            to = EX - 1 - d if side else CX + d
            for z, layer in places:
                outs[f][z, to:to + 1, :CY] = wide[layer:layer + 1]

    high, low = yh_ref[...], yl_ref[...]
    for z in range(CZ):
        src = source_of(z, gz)
        for f in range(3):
            main(f, z, f_in[f, pl.ds(src, 1)][0], high, low, z)
    sides = ((xh_ref, x_high, FIELD_ROW), (xl_ref, x_low, FIELD_ROW))
    for t in range(len(STEPS)):
        edges(t, sides, [(z, z) for z in range(CZ)])
    high, low = yhq_ref[...], ylq_ref[...]
    first_layer = (0, 4, 7)
    for f in range(3):
        for j in range(DEPTHS[f]):
            main(f, CZ + j, q_ref[first_layer[f] + j], high, low, CZ - 1 - j)
    sides = ((xhq_ref, x_high, 0), (xlq_ref, x_low, 0))
    for t, (f, d) in enumerate(STEPS):
        edges(t, sides, [(CZ + j, CZ - 1 - j) for j in range(DEPTHS[f])])

    for z in range(11):
        k = k_ref[z]
        wy_ref[z] = harmonic(k, y_next(k))
        wx_ref[z] = harmonic(k, x_next(k))
        wz_ref[z] = harmonic(k, k_ref[z + 1])
    for z in range(11):
        wy, wx = wy_ref[z], wx_ref[z]
        diag = st_ref[z] + wy + y_prev(wy) + wx + x_prev(wx) + wz_ref[z]
        if z:
            diag = diag + wz_ref[z - 1]
        inverse = RELAXATION / jnp.maximum(diag, 1e-3)
        dg_ref[z] = diag
        iv_ref[z] = inverse
        first_ref[z] = inverse * r_ref[z]

    def at(z, ref):
        return apply_at(z, ref[z], ref[z + 1], ref[z - 1] if z else None, dg_ref[z], wx_ref[z],
                        wy_ref[z], wz_ref[z], wz_ref[z - 1] if z else None)

    for z in range(10):
        s_ref[z] = first_ref[z] + iv_ref[z] * (r_ref[z] - at(z, first_ref))
    for z in range(9):
        u_ref[z] = at(z, s_ref)

    def set_row(row, value):
        acc_ref[8 * row:8 * row + 8, :] = value

    def layers(products):
        total = None
        for z in range(CZ):
            total = products(z) if total is None else total + products(z)
        return fold(total)

    def own(ref, z):
        return ref[z, :CX, :CY]

    def basis(a, z):
        return b_ref[a, pl.ds(source_of(z, gz), 1)][0]

    acc_ref[8 * ROW_RS:8 * ROW_G, :] = jnp.zeros((8 * (ROW_G - ROW_RS), 128), jnp.float32)
    acc_ref[8 * (ROW_H + 8):2048, :] = jnp.zeros((2048 - 8 * (ROW_H + 8), 128), jnp.float32)
    set_row(ROW_RS, layers(lambda z: own(r_ref, z) * own(s_ref, z)))
    set_row(ROW_SAS, layers(lambda z: own(u_ref, z) * own(s_ref, z)))
    for a in range(8):
        set_row(ROW_H + a, layers(lambda z: basis(a, z) * own(u_ref, z)))
    acc_ref[8 * ROW_G:8 * (ROW_G + 8), :] = part_ref[8 * 36:8 * 44, :]

    odd = (lane16 < 16) & (lax.rem(lane16, 2) == 1)
    group = lane8 // 16

    def y_weight(own_ref, beside_ref, inside):
        weight = harmonic(own_ref[...][:CX, :128], beside_ref[...][:CX, :128] * inside)
        weight = jnp.where(odd, pltpu.roll(weight, 128 - FACE_LANE, 1), 0.0)
        for shift in (16, 32, 64):
            weight = weight + pltpu.roll(weight, shift, 1)
        return weight

    def turned(v, d):
        return pltpu.roll(v, 128 - 16 * d, 1) if d else v

    mine = ys_hi_ref[...][:CX, 128:]
    first_mine = pltpu.roll(ys_lo_ref[...][:CX, 128:], 1, 1)
    theirs = pltpu.roll(yh_ref[...][:CX, 128:], 1, 1)
    weighted = y_weight(ys_hi_ref, yh_ref, y_high) * mine
    first_weighted = y_weight(ys_lo_ref, yl_ref, y_low) * first_mine
    face_y = {}
    for d in range(8):
        product = -weighted * turned(theirs, d)
        product = product[:8] + product[8:]
        for a in range(8):
            set_row(ROW_Y + 8 * ((a + d) % 8) + a, jnp.where(group == a, product, 0.0))
        if d < 5:
            inner = weighted * turned(mine, d) + first_weighted * turned(first_mine, d)
            face_y[d] = inner[:8] + inner[8:]

    wz_face = own(wz_ref, CZ - 1)
    wx_face = harmonic(hi_ref[FIELD_ROW:FIELD_ROW + 8, :], xh_ref[FIELD_ROW:FIELD_ROW + 8, :] * x_high)
    wx_first = harmonic(lo_ref[FIELD_ROW:FIELD_ROW + 8, :], xl_ref[FIELD_ROW:FIELD_ROW + 8, :] * x_low)
    for a in range(8):
        za = wz_face * basis(a, CZ - 1)
        xa = wx_face * hi_ref[16 * a:16 * a + 8, :]
        xa_first = wx_first * lo_ref[16 * a:16 * a + 8, :]
        for b in range(8):
            row = 8 * b + a
            set_row(ROW_Z + row, -fold(za * q_ref[10 + 2 * b]))
            x = xa * xh_ref[16 * b:16 * b + 8, :]
            set_row(ROW_X + row, -(x[:, :128] + x[:, 128:]))
            if b < a:
                continue
            x = xa * hi_ref[16 * b:16 * b + 8, :] + xa_first * lo_ref[16 * b:16 * b + 8, :]
            pair = PAIRS.index((a, b))
            value = part_ref[8 * pair:8 * pair + 8, :] + fold(za * basis(b, CZ - 1)) + x[:, :128] + x[:, 128:]
            d, place = (b - a, a) if b - a < 5 else (a - b + 8, b)
            set_row(ROW_OWN + pair, value + jnp.where(group == place, face_y[d], 0.0))

    total = acc_ref[pl.ds(0, 256, stride=8), :]
    for sub in range(1, 8):
        total = total + acc_ref[pl.ds(sub, 256, stride=8), :]
    summed = lax.dot_general(jnp.ones((8, 128), jnp.float32), total, (((1,), (1,)), ((), ())),
                             precision=HIGHEST, preferred_element_type=jnp.float32)
    pay_ref[0:1, :] = summed[0:1, :128]
    pay_ref[1:2, :] = summed[0:1, 128:]


def total_of(v):
    v = jnp.sum(v, axis=0, keepdims=True)
    if v.shape[1] == 256:
        v = v[:, :128] + v[:, 128:]
    return jnp.sum(v, axis=1, keepdims=True)


def dot(left, right):
    v = left * right
    return total_of(v[:, :128] + v[:, 128:])


def coarse_solve(tile_ref, lane_even):
    def partner(c):
        return jnp.where(lane_even, pltpu.roll(c, NDEV - 1, 1), pltpu.roll(c, 1, 1))

    def apply_e(c):
        shifted = [c, partner(c), pltpu.roll(c, NDEV - 2, 1), pltpu.roll(c, NDEV - 16, 1),
                   pltpu.roll(c, 2, 1), pltpu.roll(c, 16, 1)]
        total = None
        for o, v in enumerate(shifted):
            part = None
            for b in range(8):
                tile = (tile_ref[8 * (8 * o + b):8 * (8 * o + b) + 8, :])
                term = tile * v[b:b + 1, :]
                part = term if part is None else part + term
            total = part if total is None else total + part
        return total

    def solve(g):
        remainder, search, image = g, g, apply_e(g)
        current, along = dot(g, g), dot(g, image)
        solution = jnp.zeros_like(g)
        for iteration in range(KITERS):
            step = current / along
            solution = solution + step * search
            remainder = remainder - step * image
            if iteration == KITERS - 1:
                break
            applied = apply_e(remainder)
            updated = dot(remainder, remainder)
            ratio = updated / current
            along = dot(remainder, applied) + ratio * (2.0 * dot(remainder, image) + ratio * along)
            search = remainder + ratio * search
            image = applied + ratio * image
            current = updated
        return solution, g - remainder

    return solve


def coarse_kernel(pos_ref, gath_ref, r_ref, b_ref, q_in, xh_ref, xl_ref, xhq_ref, xlq_ref,
                  yh_ref, yl_ref, yhq_ref, ylq_ref, wx_ref, wy_ref, wz_ref, dg_ref, iv_ref, s_ref, u_ref,
                  sol_ref, res_ref, pre_ref, refined_ref, part_ref, scal_ref,
                  t_ref, tile_ref, pc_ref, q_ref):
    gz = pos_ref[2]
    dev = (pos_ref[0] * 8 + pos_ref[1]) * 2 + gz
    turned = gath_ref[...].T
    t_ref[0] = turned[:, :128]
    t_ref[1] = turned[:, 128:]

    def rows_at(index):
        return jnp.concatenate([t_ref[0, index, :], t_ref[1, index, :]], axis=1)

    for b in range(8):
        for a in range(8):
            row = ROW_OWN + PAIRS.index((min(a, b), max(a, b)))
            tile_ref[8 * b + a:8 * b + a + 1, :] = turned[row:row + 1, :]
    tile_ref[64:256, :] = turned[0:192, :]
    for b in range(8):
        tile_ref[256 + 8 * b:264 + 8 * b, :] = pltpu.roll(rows_at(pl.ds(ROW_Y + b, 8, stride=8)), 2, 1)
        tile_ref[320 + 8 * b:328 + 8 * b, :] = pltpu.roll(rows_at(pl.ds(ROW_X + b, 8, stride=8)), 16, 1)
    lane = lax.broadcasted_iota(jnp.int32, (8, NDEV), 1)
    solve = coarse_solve(tile_ref, lax.rem(lane, 2) == 0)
    g = turned[ROW_G:ROW_G + 8]
    h = turned[ROW_H:ROW_H + 8]
    rs = turned[ROW_RS:ROW_RS + 1]
    sas = turned[ROW_SAS:ROW_SAS + 1]
    c1, ec1 = solve(g)
    rz = total_of(rs) + dot(g, c1)
    curvature = total_of(sas) + dot(2.0 * h + ec1, c1)
    step = rz / curvature
    g2 = g - step * (h + ec1)
    c2, _ = solve(g2)
    g2c2 = dot(g2, c2)

    own_c = pltpu.roll(c1, lax.rem(NDEV - dev, NDEV), 1)
    other = dev + 1 - 2 * gz
    other_c = pltpu.roll(c1, lax.rem(NDEV - other, NDEV), 1)

    def at_lane(c, index):
        return c[:, index % NDEV:index % NDEV + 1]

    def spread(vectors, c):
        total = None
        for a, v in enumerate(vectors):
            term = v * c[a:a + 1, :]
            total = term if total is None else total + term
        return total

    mine, theirs = at_lane(own_c, 0), at_lane(other_c, 0)
    for z in range(CZ):
        pc_ref[z, :CX, :CY] = spread([b_ref[a, pl.ds(source_of(z, gz), 1)][0] for a in range(8)], mine)
    for j in range(2):
        pc_ref[CZ + j, :CX, :CY] = spread([q_in[10 + 2 * a + j] for a in range(8)], theirs)
    for z in range(10):
        pc_ref[z, CX:, :CY] = jnp.zeros((EX - CX, CY), jnp.float32)
    for step_x, ref, other in ((16, xh_ref, xhq_ref), (-16, xl_ref, xlq_ref)):
        for d in range(2):
            rows = spread([ref[16 * a + 8 * d:16 * a + 8 * d + 8, :] for a in range(8)], at_lane(own_c, step_x))
            to = CX + d if step_x > 0 else EX - 1 - d
            for z in range(CZ):
                pc_ref[z, to:to + 1, :CY] = rows[z:z + 1]
        to = CX if step_x > 0 else EX - 1
        last = other[LAST_ROW - FIELD_ROW:LAST_ROW - FIELD_ROW + 8, :] * at_lane(other_c, step_x)
        pc_ref[CZ, to:to + 1, :CY] = jnp.sum(last, axis=0, keepdims=True)

    lane24 = lax.broadcasted_iota(jnp.int32, (EX, 128), 1)
    row24 = lax.broadcasted_iota(jnp.int32, (EX, 128), 0)

    def by_group(c):
        total = jnp.zeros((EX, 128), jnp.float32)
        for a in range(8):
            total = jnp.where(lane24 // 16 == a, c[a:a + 1, :], total)
        return total

    def columns(ref, c, step_y, corners):
        high_x = low_x = 0.0
        if corners:
            high_x, low_x = by_group(at_lane(c, 16 + step_y)), by_group(at_lane(c, step_y - 16))
        v = jnp.where(row24 < CX, by_group(at_lane(c, step_y)), jnp.where(row24 < CX + 4, high_x, low_x))
        v = v * ref[...][:, 128:]
        for shift in (64, 32, 16):
            v = v + pltpu.roll(v, shift, 1)
        return v

    def place_columns(z, high, low, layer):
        pc_ref[z, :, CY:] = jnp.where(lane24 < 2, pltpu.roll(high, (-2 * layer) % 128, 1), jnp.where(
            lane24 >= 126, pltpu.roll(low, (126 - 2 * layer) % 128, 1), 0.0))

    high, low = columns(yh_ref, own_c, 2, True), columns(yl_ref, own_c, -2, True)
    for z in range(CZ):
        place_columns(z, high, low, z)
    high, low = columns(yhq_ref, other_c, 2, False), columns(ylq_ref, other_c, -2, False)
    for j in range(2):
        place_columns(CZ + j, high, low, CZ - 1 - j)

    def at(z, ref):
        return apply_at(z, ref[z], ref[z + 1], ref[z - 1] if z else None, dg_ref[z], wx_ref[z],
                        wy_ref[z], wz_ref[z], wz_ref[z - 1] if z else None)

    def out_z(z):
        return z + gz * (CZ - 1 - 2 * z)

    def keep(ref, z, value):
        ref[pl.ds(out_z(z), 1)] = value[None, :CX, :CY]

    for z in range(9):
        image = u_ref[z] + at(z, pc_ref)
        residual = r_ref[z] - step * image
        q_ref[z] = iv_ref[z] * residual
        if z < CZ:
            keep(res_ref, z, residual)
            pre = s_ref[z, :CX, :CY] + pc_ref[z, :CX, :CY]
            keep(pre_ref, z, pre)
            keep(sol_ref, z, step * pre)
    own_c2 = pltpu.roll(c2, lax.rem(NDEV - dev, NDEV), 1)
    partial = jnp.zeros((8, 128), jnp.float32)
    for z in range(CZ):
        residual = res_ref[pl.ds(out_z(z), 1)][0]
        second = q_ref[z, :CX, :CY] + iv_ref[z, :CX, :CY] * (residual - at(z, q_ref)[:CX, :CY])
        partial = partial + fold(residual * second)
        for b in range(8):
            second = second + b_ref[b, pl.ds(out_z(z), 1)][0] * own_c2[b:b + 1, 0:1]
        keep(refined_ref, z, second)
    part_ref[...] = jnp.sum(partial, axis=0, keepdims=True)
    spot = lax.broadcasted_iota(jnp.int32, (1, 128), 1)
    scal_ref[...] = jnp.where(spot == 0, g2c2, rz)


def call(kernel, out_shapes, scratch, n_args, smem_first=False):
    whole = pl.BlockSpec(memory_space=pltpu.VMEM)
    specs = [whole] * n_args
    if smem_first:
        specs[0] = pl.BlockSpec(memory_space=pltpu.SMEM)
    return pl.pallas_call(
        kernel,
        out_shape=[jax.ShapeDtypeStruct(s, jnp.float32) for s in out_shapes],
        in_specs=specs,
        out_specs=[whole] * len(out_shapes),
        scratch_shapes=[pltpu.VMEM(s, jnp.float32) for s in scratch],
        compiler_params=pltpu.CompilerParams(vmem_limit_bytes=VMEM_LIMIT),
    )


def ring(axis, to):
    n = lax.axis_size(axis)
    return [(i, (i + to) % n) for i in range(n)]


def gather_rows(row):
    rows = jnp.broadcast_to(row[None], (NDEV,) + row.shape)
    return lax.all_to_all(rows, AXES, 0, 0, tiled=False)


def local(right_side, conductivity, storage, basis):
    pos = jnp.stack([lax.axis_index(a) for a in AXES]).astype(jnp.int32)
    swap = [(0, 1), (1, 0)]

    def exchange(axis, hi, lo):
        return lax.ppermute(lo, axis, ring(axis, -1)), lax.ppermute(hi, axis, ring(axis, 1))

    box, faces = (CZ, CX, CY), (CORNER_ROW, CY)
    fields = jnp.stack([conductivity, storage, right_side])
    b = basis.astype(jnp.float32)
    main_hi, main_lo = call(pack_y_kernel, [(CX, 256)] * 2, [], 3, True)(pos, fields, b)
    main_high, main_low = exchange("gy", main_hi, main_lo)
    hi, lo, layers = call(pack_x_kernel, [faces, faces, (26, CX, CY)], [], 3, True)(pos, fields, b)
    other_layers = lax.ppermute(layers, "gz", swap)
    hi = jnp.concatenate([hi, main_high[CX - 4:], main_low[CX - 4:]], axis=0)
    lo = jnp.concatenate([lo, main_high[:4], main_low[:4]], axis=0)
    hi, lo, main_high, main_low, gate = lax.optimization_barrier((hi, lo, main_high, main_low, pos))
    x_high, x_low = exchange("gx", hi, lo)
    other_main = lax.ppermute(jnp.concatenate([main_high, main_low], axis=0), "gz", swap)
    part, = call(gram_kernel, [(44 * 8, 128)], [], 3, True)(gate, fields, b)
    x_high, x_low, other_layers, other_main, part = lax.optimization_barrier(
        (x_high, x_low, other_layers, other_main, part))
    other_xh = lax.ppermute(x_high[FIELD_ROW:], "gz", swap)
    other_xl = lax.ppermute(x_low[FIELD_ROW:], "gz", swap)

    def with_corners(main, high, low, row):
        return jnp.concatenate([main, high[row:row + 4], low[row:row + 4]], axis=0)

    y_high = with_corners(main_high, x_high, x_low, CORNER_ROW)
    y_low = with_corners(main_low, x_high, x_low, CORNER_ROW + 4)
    other_yh = with_corners(other_main[:CX], other_xh, other_xl, CORNER_ROW - FIELD_ROW)
    other_yl = with_corners(other_main[CX:], other_xh, other_xl, CORNER_ROW - FIELD_ROW + 4)

    ext = (EZ, EX, EY)
    pay, r_ext, wx, wy, wz, dg, iv, s, u = call(
        prepare_kernel, [(2, 128)] + [ext] * 8, [ext, ext, ext, (2048, 128)], 17, True,
    )(pos, fields, part, b, other_layers, hi, lo, x_high, x_low, other_xh, other_xl,
      main_hi, main_lo, y_high, y_low, other_yh, other_yl)
    gathered = gather_rows(pay).reshape(NDEV, 256)
    sol, res, pre, refined, total, scal = call(
        coarse_kernel, [box] * 4 + [(1, 128)] * 2,
        [(2, 256, 128), (384, 256), ext, ext], 20, True,
    )(pos, gathered, r_ext, b, other_layers, x_high, x_low, other_xh, other_xl,
      y_high, y_low, other_yh, other_yl, wx, wy, wz, dg, iv, s, u)
    growth = (jnp.sum(gather_rows(total)) + scal[0, 0]) / scal[0, 1]
    direction = refined + growth * pre
    return sol, res, direction


def solution(mesh):
    spec = P("gz", "gx", "gy")
    return jax.shard_map(
        local,
        mesh=mesh,
        in_specs=(spec, spec, spec, P(None, "gz", "gx", "gy")),
        out_specs=(spec, spec, spec),
        check_vma=False,
    )
```

```python
import functools

import jax
import jax.numpy as jnp
from jax import lax
from jax.experimental import pallas as pl
from jax.experimental.pallas import tpu as pltpu
from jax.sharding import PartitionSpec as P

KITERS = 6
RELAXATION = 0.6
HIGHEST = lax.Precision.HIGHEST
AXES = ("gx", "gy", "gz")
CZ, CX, CY = 8, 16, 256
EZ, EX, EY = 12, 24, 384
NDEV = 256
PAIRS = [(a, b) for a in range(8) for b in range(a, 8)]
ROW_Z, ROW_Y, ROW_X, ROW_OWN, ROW_RS, ROW_SAS, ROW_G, ROW_H = 0, 64, 128, 192, 228, 229, 232, 240
DEPTHS = (4, 3, 3)
STEPS = [(f, d) for f in range(3) for d in range(DEPTHS[f])]
FIELD_ROW, LAST_ROW, CORNER_ROW = 128, 208, 216
FACE_LANE = 96
VMEM_LIMIT = 24 * 1024 * 1024


def harmonic(k, other):
    return 2.0 * k * other / jnp.maximum(k + other, 1e-30)


def y_next(v):
    return pltpu.roll(v, v.shape[1] - 1, 1)


def y_prev(v):
    return pltpu.roll(v, 1, 1)


def x_next(v):
    return pltpu.roll(v, v.shape[0] - 1, 0)


def x_prev(v):
    return pltpu.roll(v, 1, 0)


def apply_at(z, v, v_up, v_down, diag, wx, wy, wz_up, wz_down):
    total = diag * v - wy * y_next(v) - y_prev(wy * v) - wx * x_next(v) - x_prev(wx * v)
    if v_up is not None:
        total = total - wz_up * v_up
    if v_down is not None:
        total = total - wz_down * v_down
    return total


def fold(v):
    return (v[:8, :128] + v[8:, :128]) + (v[:8, 128:] + v[8:, 128:])


def flag(inside):
    return jnp.where(inside, 1.0, 0.0).astype(jnp.float32)


def source_of(z, gz):
    return z + gz * (CZ - 1 - 2 * z)


def pack_x_kernel(pos_ref, f_ref, b_ref, hi_ref, lo_ref, q_ref):
    gz = pos_ref[2]
    for z in range(CZ):
        src, j = source_of(z, gz), CZ - 1 - z
        fields = [f_ref[f, pl.ds(src, 1)][0] for f in range(3)]
        for t, (f, d) in enumerate(STEPS):
            row = FIELD_ROW + 8 * t + z
            hi_ref[row:row + 1, :] = fields[f][CX - 1 - d:CX - d]
            lo_ref[row:row + 1, :] = fields[f][d:d + 1]
        if j < 4:
            q_ref[j] = fields[0]
        if j < 3:
            q_ref[4 + j] = fields[1]
            q_ref[7 + j] = fields[2]
        for a in range(8):
            v = b_ref[a, pl.ds(src, 1)][0]
            for d in range(2):
                row = 16 * a + 8 * d + z
                hi_ref[row:row + 1, :] = v[CX - 1 - d:CX - d]
                lo_ref[row:row + 1, :] = v[d:d + 1]
            if j == 0:
                hi_ref[LAST_ROW + a:LAST_ROW + a + 1, :] = v[CX - 1:CX]
                lo_ref[LAST_ROW + a:LAST_ROW + a + 1, :] = v[0:1]
            if j < 2:
                q_ref[10 + 2 * a + j] = v


def pack_y_kernel(pos_ref, f_ref, b_ref, hi_ref, lo_ref):
    gz = pos_ref[2]
    lane = lax.broadcasted_iota(jnp.int32, (CX, 128), 1)
    hi = [jnp.zeros((CX, 128), jnp.float32)] * 2
    lo = [jnp.zeros((CX, 128), jnp.float32)] * 2

    def put(half, v, width, offset):
        mask = (lane >= offset) & (lane < offset + width)
        hi[half] = jnp.where(mask, pltpu.roll(v[:, 128:], (offset + width) % 128, 1), hi[half])
        lo[half] = jnp.where(mask, pltpu.roll(v[:, :128], offset, 1), lo[half])

    for z in range(CZ):
        src = source_of(z, gz)
        for f in range(3):
            v = f_ref[f, pl.ds(src, 1)][0]
            put(0, v, 4, 32 * f + 4 * z)
            if f == 0:
                put(0, v, 1, FACE_LANE + 2 * z + 1)
        for a in range(8):
            put(1, b_ref[a, pl.ds(src, 1)][0], 2, 16 * a + 2 * z)
    for half in range(2):
        hi_ref[:, 128 * half:128 * half + 128] = hi[half]
        lo_ref[:, 128 * half:128 * half + 128] = lo[half]


def gram_kernel(pos_ref, f_ref, b_ref, part_ref):
    gz = pos_ref[2]
    part_ref[...] = jnp.zeros_like(part_ref)
    rows = lax.broadcasted_iota(jnp.int32, (CX, CY), 0)
    lanes = lax.broadcasted_iota(jnp.int32, (CX, CY), 1)

    def add(row, value):
        part_ref[8 * row:8 * row + 8, :] += value

    def body(z, carry):
        src, up, down = source_of(z, gz), jnp.minimum(z + 1, CZ - 1), jnp.maximum(z - 1, 0)
        k, st, r = (f_ref[f, pl.ds(src, 1)][0] for f in range(3))
        src_up, src_down = source_of(up, gz), source_of(down, gz)
        wy = jnp.where(lanes == CY - 1, 0.0, harmonic(k, y_next(k)))
        wx = jnp.where(rows == CX - 1, 0.0, harmonic(k, x_next(k)))
        wz_up = jnp.where(z < CZ - 1, harmonic(k, f_ref[0, pl.ds(src_up, 1)][0]), 0.0)
        wz_down = jnp.where(z > 0, harmonic(k, f_ref[0, pl.ds(src_down, 1)][0]), 0.0)
        diag = st + wy + y_prev(wy) + wx + x_prev(wx) + wz_up + wz_down
        basis = [b_ref[a, pl.ds(src, 1)][0] for a in range(8)]
        for b in range(8):
            add(36 + b, fold(basis[b] * r))
            image = apply_at(z, basis[b], b_ref[b, pl.ds(src_up, 1)][0],
                             b_ref[b, pl.ds(src_down, 1)][0], diag,
                             wx, wy, wz_up, wz_down)
            for a in range(b + 1):
                add(PAIRS.index((a, b)), fold(basis[a] * image))
        return carry

    lax.fori_loop(0, CZ, body, 0)


def prepare_kernel(pos_ref, f_in, part_ref, b_ref, q_ref, hi_ref, lo_ref, xh_ref, xl_ref, xhq_ref,
                   xlq_ref, ys_hi_ref, ys_lo_ref, yh_ref, yl_ref, yhq_ref, ylq_ref,
                   pay_ref, r_ref, wx_ref, wy_ref, wz_ref, dg_ref, iv_ref, s_ref, u_ref,
                   k_ref, st_ref, first_ref, acc_ref):
    gx, gy, gz = pos_ref[0], pos_ref[1], pos_ref[2]
    x_high, x_low = flag(gx < 15), flag(gx > 0)
    y_high, y_low = flag(gy < 7), flag(gy > 0)
    lane16 = lax.broadcasted_iota(jnp.int32, (CX, 128), 1)
    lane8 = lax.broadcasted_iota(jnp.int32, (8, 128), 1)
    lane24 = lax.broadcasted_iota(jnp.int32, (EX, 128), 1)
    row24 = lax.broadcasted_iota(jnp.int32, (EX, 128), 0)
    inside_x = jnp.where(row24 < CX, 1.0, jnp.where(row24 < CX + 4, x_high, x_low))
    outs = (k_ref, st_ref, r_ref)

    def main(f, z, value, high, low, layer):
        ref, offset = outs[f], 32 * f + 4 * layer
        high = pltpu.roll(high[:, :128], -offset % 128, 1)
        low = pltpu.roll(low[:, :128], (124 - offset) % 128, 1)
        if f == 0:
            high, low = high * (inside_x * y_high), low * (inside_x * y_low)
        ref[z, :CX, :CY] = value
        ref[z, :, CY:] = jnp.where(lane24 < 4, high, jnp.where(lane24 >= 124, low, 1.0))
        if f:
            ref[z, CX:, :CY] = jnp.ones((EX - CX, CY), jnp.float32)

    def edges(t, sides, places):
        f, d = STEPS[t]
        for side, (ref, inside, row) in enumerate(sides):
            wide = ref[row + 8 * t:row + 8 * t + 8, :]
            if f == 0:
                wide = wide * inside
            to = EX - 1 - d if side else CX + d
            for z, layer in places:
                outs[f][z, to:to + 1, :CY] = wide[layer:layer + 1]

    high, low = yh_ref[...], yl_ref[...]
    for z in range(CZ):
        src = source_of(z, gz)
        for f in range(3):
            main(f, z, f_in[f, pl.ds(src, 1)][0], high, low, z)
    sides = ((xh_ref, x_high, FIELD_ROW), (xl_ref, x_low, FIELD_ROW))
    for t in range(len(STEPS)):
        edges(t, sides, [(z, z) for z in range(CZ)])
    high, low = yhq_ref[...], ylq_ref[...]
    first_layer = (0, 4, 7)
    for f in range(3):
        for j in range(DEPTHS[f]):
            main(f, CZ + j, q_ref[first_layer[f] + j], high, low, CZ - 1 - j)
    sides = ((xhq_ref, x_high, 0), (xlq_ref, x_low, 0))
    for t, (f, d) in enumerate(STEPS):
        edges(t, sides, [(CZ + j, CZ - 1 - j) for j in range(DEPTHS[f])])

    for z in range(11):
        k = k_ref[z]
        wy_ref[z] = harmonic(k, y_next(k))
        wx_ref[z] = harmonic(k, x_next(k))
        wz_ref[z] = harmonic(k, k_ref[z + 1])
    for z in range(11):
        wy, wx = wy_ref[z], wx_ref[z]
        diag = st_ref[z] + wy + y_prev(wy) + wx + x_prev(wx) + wz_ref[z]
        if z:
            diag = diag + wz_ref[z - 1]
        inverse = RELAXATION / jnp.maximum(diag, 1e-3)
        dg_ref[z] = diag
        iv_ref[z] = inverse
        first_ref[z] = inverse * r_ref[z]

    def at(z, ref):
        return apply_at(z, ref[z], ref[z + 1], ref[z - 1] if z else None, dg_ref[z], wx_ref[z],
                        wy_ref[z], wz_ref[z], wz_ref[z - 1] if z else None)

    for z in range(10):
        s_ref[z] = first_ref[z] + iv_ref[z] * (r_ref[z] - at(z, first_ref))
    for z in range(9):
        u_ref[z] = at(z, s_ref)

    def set_row(row, value):
        acc_ref[8 * row:8 * row + 8, :] = value

    def layers(products):
        total = None
        for z in range(CZ):
            total = products(z) if total is None else total + products(z)
        return fold(total)

    def own(ref, z):
        return ref[z, :CX, :CY]

    def basis(a, z):
        return b_ref[a, pl.ds(source_of(z, gz), 1)][0]

    acc_ref[8 * ROW_RS:8 * ROW_G, :] = jnp.zeros((8 * (ROW_G - ROW_RS), 128), jnp.float32)
    acc_ref[8 * (ROW_H + 8):2048, :] = jnp.zeros((2048 - 8 * (ROW_H + 8), 128), jnp.float32)
    set_row(ROW_RS, layers(lambda z: own(r_ref, z) * own(s_ref, z)))
    set_row(ROW_SAS, layers(lambda z: own(u_ref, z) * own(s_ref, z)))
    for a in range(8):
        set_row(ROW_H + a, layers(lambda z: basis(a, z) * own(u_ref, z)))
    acc_ref[8 * ROW_G:8 * (ROW_G + 8), :] = part_ref[8 * 36:8 * 44, :]

    odd = (lane16 < 16) & (lax.rem(lane16, 2) == 1)
    group = lane8 // 16

    def y_weight(own_ref, beside_ref, inside):
        weight = harmonic(own_ref[...][:CX, :128], beside_ref[...][:CX, :128] * inside)
        weight = jnp.where(odd, pltpu.roll(weight, 128 - FACE_LANE, 1), 0.0)
        for shift in (16, 32, 64):
            weight = weight + pltpu.roll(weight, shift, 1)
        return weight

    def turned(v, d):
        return pltpu.roll(v, 128 - 16 * d, 1) if d else v

    mine = ys_hi_ref[...][:CX, 128:]
    first_mine = pltpu.roll(ys_lo_ref[...][:CX, 128:], 1, 1)
    theirs = pltpu.roll(yh_ref[...][:CX, 128:], 1, 1)
    weighted = y_weight(ys_hi_ref, yh_ref, y_high) * mine
    first_weighted = y_weight(ys_lo_ref, yl_ref, y_low) * first_mine
    face_y = {}
    for d in range(8):
        product = -weighted * turned(theirs, d)
        product = product[:8] + product[8:]
        for a in range(8):
            set_row(ROW_Y + 8 * ((a + d) % 8) + a, jnp.where(group == a, product, 0.0))
        if d < 5:
            inner = weighted * turned(mine, d) + first_weighted * turned(first_mine, d)
            face_y[d] = inner[:8] + inner[8:]

    wz_face = own(wz_ref, CZ - 1)
    wx_face = harmonic(hi_ref[FIELD_ROW:FIELD_ROW + 8, :], xh_ref[FIELD_ROW:FIELD_ROW + 8, :] * x_high)
    wx_first = harmonic(lo_ref[FIELD_ROW:FIELD_ROW + 8, :], xl_ref[FIELD_ROW:FIELD_ROW + 8, :] * x_low)
    for a in range(8):
        za = wz_face * basis(a, CZ - 1)
        xa = wx_face * hi_ref[16 * a:16 * a + 8, :]
        xa_first = wx_first * lo_ref[16 * a:16 * a + 8, :]
        for b in range(8):
            row = 8 * b + a
            set_row(ROW_Z + row, -fold(za * q_ref[10 + 2 * b]))
            x = xa * xh_ref[16 * b:16 * b + 8, :]
            set_row(ROW_X + row, -(x[:, :128] + x[:, 128:]))
            if b < a:
                continue
            x = xa * hi_ref[16 * b:16 * b + 8, :] + xa_first * lo_ref[16 * b:16 * b + 8, :]
            pair = PAIRS.index((a, b))
            value = part_ref[8 * pair:8 * pair + 8, :] + fold(za * basis(b, CZ - 1)) + x[:, :128] + x[:, 128:]
            d, place = (b - a, a) if b - a < 5 else (a - b + 8, b)
            set_row(ROW_OWN + pair, value + jnp.where(group == place, face_y[d], 0.0))

    total = acc_ref[pl.ds(0, 256, stride=8), :]
    for sub in range(1, 8):
        total = total + acc_ref[pl.ds(sub, 256, stride=8), :]
    summed = lax.dot_general(jnp.ones((8, 128), jnp.float32), total, (((1,), (1,)), ((), ())),
                             precision=HIGHEST, preferred_element_type=jnp.float32)
    pay_ref[0:1, :] = summed[0:1, :128]
    pay_ref[1:2, :] = summed[0:1, 128:]


def total_of(v):
    v = jnp.sum(v, axis=0, keepdims=True)
    if v.shape[1] == 256:
        v = v[:, :128] + v[:, 128:]
    return jnp.sum(v, axis=1, keepdims=True)


def dot(left, right):
    v = left * right
    return total_of(v[:, :128] + v[:, 128:])


def coarse_solve(tile_ref, lane_even):
    def partner(c):
        return jnp.where(lane_even, pltpu.roll(c, NDEV - 1, 1), pltpu.roll(c, 1, 1))

    def apply_e(c):
        shifted = [c, partner(c), pltpu.roll(c, NDEV - 2, 1), pltpu.roll(c, NDEV - 16, 1),
                   pltpu.roll(c, 2, 1), pltpu.roll(c, 16, 1)]
        total = None
        for o, v in enumerate(shifted):
            part = None
            for b in range(8):
                tile = (tile_ref[8 * (8 * o + b):8 * (8 * o + b) + 8, :])
                term = tile * v[b:b + 1, :]
                part = term if part is None else part + term
            total = part if total is None else total + part
        return total

    def solve(g):
        remainder, search, image = g, g, apply_e(g)
        current, along = dot(g, g), dot(g, image)
        solution = jnp.zeros_like(g)
        for iteration in range(KITERS):
            step = current / along
            solution = solution + step * search
            remainder = remainder - step * image
            if iteration == KITERS - 1:
                break
            applied = apply_e(remainder)
            updated = dot(remainder, remainder)
            ratio = updated / current
            along = dot(remainder, applied) + ratio * (2.0 * dot(remainder, image) + ratio * along)
            search = remainder + ratio * search
            image = applied + ratio * image
            current = updated
        return solution, g - remainder

    return solve


def coarse_kernel(pos_ref, gath_ref, r_ref, b_ref, q_in, xh_ref, xl_ref, xhq_ref, xlq_ref,
                  yh_ref, yl_ref, yhq_ref, ylq_ref, wx_ref, wy_ref, wz_ref, dg_ref, iv_ref, s_ref, u_ref,
                  sol_ref, res_ref, pre_ref, refined_ref, part_ref, scal_ref,
                  t_ref, tile_ref, pc_ref, q_ref):
    gz = pos_ref[2]
    dev = (pos_ref[0] * 8 + pos_ref[1]) * 2 + gz
    turned = gath_ref[...].T
    t_ref[0] = turned[:, :128]
    t_ref[1] = turned[:, 128:]

    def rows_at(index):
        return jnp.concatenate([t_ref[0, index, :], t_ref[1, index, :]], axis=1)

    for b in range(8):
        for a in range(8):
            row = ROW_OWN + PAIRS.index((min(a, b), max(a, b)))
            tile_ref[8 * b + a:8 * b + a + 1, :] = turned[row:row + 1, :]
    tile_ref[64:256, :] = turned[0:192, :]
    for b in range(8):
        tile_ref[256 + 8 * b:264 + 8 * b, :] = pltpu.roll(rows_at(pl.ds(ROW_Y + b, 8, stride=8)), 2, 1)
        tile_ref[320 + 8 * b:328 + 8 * b, :] = pltpu.roll(rows_at(pl.ds(ROW_X + b, 8, stride=8)), 16, 1)
    lane = lax.broadcasted_iota(jnp.int32, (8, NDEV), 1)
    solve = coarse_solve(tile_ref, lax.rem(lane, 2) == 0)
    g = turned[ROW_G:ROW_G + 8]
    h = turned[ROW_H:ROW_H + 8]
    rs = turned[ROW_RS:ROW_RS + 1]
    sas = turned[ROW_SAS:ROW_SAS + 1]
    c1, ec1 = solve(g)
    rz = total_of(rs) + dot(g, c1)
    curvature = total_of(sas) + dot(2.0 * h + ec1, c1)
    step = rz / curvature
    g2 = g - step * (h + ec1)
    c2, _ = solve(g2)
    g2c2 = dot(g2, c2)

    own_c = pltpu.roll(c1, lax.rem(NDEV - dev, NDEV), 1)
    other = dev + 1 - 2 * gz
    other_c = pltpu.roll(c1, lax.rem(NDEV - other, NDEV), 1)

    def at_lane(c, index):
        return c[:, index % NDEV:index % NDEV + 1]

    def spread(vectors, c):
        total = None
        for a, v in enumerate(vectors):
            term = v * c[a:a + 1, :]
            total = term if total is None else total + term
        return total

    mine, theirs = at_lane(own_c, 0), at_lane(other_c, 0)
    for z in range(CZ):
        pc_ref[z, :CX, :CY] = spread([b_ref[a, pl.ds(source_of(z, gz), 1)][0] for a in range(8)], mine)
    for j in range(2):
        pc_ref[CZ + j, :CX, :CY] = spread([q_in[10 + 2 * a + j] for a in range(8)], theirs)
    for z in range(10):
        pc_ref[z, CX:, :CY] = jnp.zeros((EX - CX, CY), jnp.float32)
    for step_x, ref, other in ((16, xh_ref, xhq_ref), (-16, xl_ref, xlq_ref)):
        for d in range(2):
            rows = spread([ref[16 * a + 8 * d:16 * a + 8 * d + 8, :] for a in range(8)], at_lane(own_c, step_x))
            to = CX + d if step_x > 0 else EX - 1 - d
            for z in range(CZ):
                pc_ref[z, to:to + 1, :CY] = rows[z:z + 1]
        to = CX if step_x > 0 else EX - 1
        last = other[LAST_ROW - FIELD_ROW:LAST_ROW - FIELD_ROW + 8, :] * at_lane(other_c, step_x)
        pc_ref[CZ, to:to + 1, :CY] = jnp.sum(last, axis=0, keepdims=True)

    lane24 = lax.broadcasted_iota(jnp.int32, (EX, 128), 1)
    row24 = lax.broadcasted_iota(jnp.int32, (EX, 128), 0)

    def by_group(c):
        total = jnp.zeros((EX, 128), jnp.float32)
        for a in range(8):
            total = jnp.where(lane24 // 16 == a, c[a:a + 1, :], total)
        return total

    def columns(ref, c, step_y, corners):
        high_x = low_x = 0.0
        if corners:
            high_x, low_x = by_group(at_lane(c, 16 + step_y)), by_group(at_lane(c, step_y - 16))
        v = jnp.where(row24 < CX, by_group(at_lane(c, step_y)), jnp.where(row24 < CX + 4, high_x, low_x))
        v = v * ref[...][:, 128:]
        for shift in (64, 32, 16):
            v = v + pltpu.roll(v, shift, 1)
        return v

    def place_columns(z, high, low, layer):
        pc_ref[z, :, CY:] = jnp.where(lane24 < 2, pltpu.roll(high, (-2 * layer) % 128, 1), jnp.where(
            lane24 >= 126, pltpu.roll(low, (126 - 2 * layer) % 128, 1), 0.0))

    high, low = columns(yh_ref, own_c, 2, True), columns(yl_ref, own_c, -2, True)
    for z in range(CZ):
        place_columns(z, high, low, z)
    high, low = columns(yhq_ref, other_c, 2, False), columns(ylq_ref, other_c, -2, False)
    for j in range(2):
        place_columns(CZ + j, high, low, CZ - 1 - j)

    def at(z, ref):
        return apply_at(z, ref[z], ref[z + 1], ref[z - 1] if z else None, dg_ref[z], wx_ref[z],
                        wy_ref[z], wz_ref[z], wz_ref[z - 1] if z else None)

    def out_z(z):
        return z + gz * (CZ - 1 - 2 * z)

    def keep(ref, z, value):
        ref[pl.ds(out_z(z), 1)] = value[None, :CX, :CY]

    for z in range(9):
        image = u_ref[z] + at(z, pc_ref)
        residual = r_ref[z] - step * image
        q_ref[z] = iv_ref[z] * residual
        if z < CZ:
            keep(res_ref, z, residual)
            pre = s_ref[z, :CX, :CY] + pc_ref[z, :CX, :CY]
            keep(pre_ref, z, pre)
            keep(sol_ref, z, step * pre)
    own_c2 = pltpu.roll(c2, lax.rem(NDEV - dev, NDEV), 1)
    partial = jnp.zeros((8, 128), jnp.float32)
    for z in range(CZ):
        residual = res_ref[pl.ds(out_z(z), 1)][0]
        second = q_ref[z, :CX, :CY] + iv_ref[z, :CX, :CY] * (residual - at(z, q_ref)[:CX, :CY])
        partial = partial + fold(residual * second)
        for b in range(8):
            second = second + b_ref[b, pl.ds(out_z(z), 1)][0] * own_c2[b:b + 1, 0:1]
        keep(refined_ref, z, second)
    part_ref[...] = jnp.sum(partial, axis=0, keepdims=True)
    spot = lax.broadcasted_iota(jnp.int32, (1, 128), 1)
    scal_ref[...] = jnp.where(spot == 0, g2c2, rz)


def finish_kernel(parts_ref, scal_ref, refined_ref, pre_ref, out_ref):
    growth = (total_of(parts_ref[...]) + scal_ref[:, 0:1]) / scal_ref[:, 1:2]
    for z in range(CZ):
        out_ref[z] = refined_ref[z] + growth * pre_ref[z]


def call(kernel, out_shapes, scratch, n_args, smem_first=False):
    whole = pl.BlockSpec(memory_space=pltpu.VMEM)
    specs = [whole] * n_args
    if smem_first:
        specs[0] = pl.BlockSpec(memory_space=pltpu.SMEM)
    return pl.pallas_call(
        kernel,
        out_shape=[jax.ShapeDtypeStruct(s, jnp.float32) for s in out_shapes],
        in_specs=specs,
        out_specs=[whole] * len(out_shapes),
        scratch_shapes=[pltpu.VMEM(s, jnp.float32) for s in scratch],
        compiler_params=pltpu.CompilerParams(vmem_limit_bytes=VMEM_LIMIT),
    )


def ring(axis, to):
    n = lax.axis_size(axis)
    return [(i, (i + to) % n) for i in range(n)]


def gather_rows(row):
    rows = jnp.broadcast_to(row[None], (NDEV,) + row.shape)
    return lax.all_to_all(rows, AXES, 0, 0, tiled=False)


def local(right_side, conductivity, storage, basis):
    pos = jnp.stack([lax.axis_index(a) for a in AXES]).astype(jnp.int32)
    swap = [(0, 1), (1, 0)]

    def exchange(axis, hi, lo):
        return lax.ppermute(lo, axis, ring(axis, -1)), lax.ppermute(hi, axis, ring(axis, 1))

    box, faces = (CZ, CX, CY), (CORNER_ROW, CY)
    fields = jnp.stack([conductivity, storage, right_side])
    b = basis.astype(jnp.float32)
    main_hi, main_lo = call(pack_y_kernel, [(CX, 256)] * 2, [], 3, True)(pos, fields, b)
    main_high, main_low = exchange("gy", main_hi, main_lo)
    hi, lo, layers = call(pack_x_kernel, [faces, faces, (26, CX, CY)], [], 3, True)(pos, fields, b)
    other_layers = lax.ppermute(layers, "gz", swap)
    hi = jnp.concatenate([hi, main_high[CX - 4:], main_low[CX - 4:]], axis=0)
    lo = jnp.concatenate([lo, main_high[:4], main_low[:4]], axis=0)
    hi, lo, main_high, main_low, gate = lax.optimization_barrier((hi, lo, main_high, main_low, pos))
    x_high, x_low = exchange("gx", hi, lo)
    other_main = lax.ppermute(jnp.concatenate([main_high, main_low], axis=0), "gz", swap)
    part, = call(gram_kernel, [(44 * 8, 128)], [], 3, True)(gate, fields, b)
    x_high, x_low, other_layers, other_main, part = lax.optimization_barrier(
        (x_high, x_low, other_layers, other_main, part))
    other_x = lax.ppermute(jnp.concatenate([x_high[FIELD_ROW:], x_low[FIELD_ROW:]], axis=0), "gz", swap)
    other_xh, other_xl = other_x[:CORNER_ROW + 8 - FIELD_ROW], other_x[CORNER_ROW + 8 - FIELD_ROW:]

    def with_corners(main, high, low, row):
        return jnp.concatenate([main, high[row:row + 4], low[row:row + 4]], axis=0)

    y_high = with_corners(main_high, x_high, x_low, CORNER_ROW)
    y_low = with_corners(main_low, x_high, x_low, CORNER_ROW + 4)
    other_yh = with_corners(other_main[:CX], other_xh, other_xl, CORNER_ROW - FIELD_ROW)
    other_yl = with_corners(other_main[CX:], other_xh, other_xl, CORNER_ROW - FIELD_ROW + 4)

    ext = (EZ, EX, EY)
    pay, r_ext, wx, wy, wz, dg, iv, s, u = call(
        prepare_kernel, [(2, 128)] + [ext] * 8, [ext, ext, ext, (2048, 128)], 17, True,
    )(pos, fields, part, b, other_layers, hi, lo, x_high, x_low, other_xh, other_xl,
      main_hi, main_lo, y_high, y_low, other_yh, other_yl)
    gathered = gather_rows(pay).reshape(NDEV, 256)
    sol, res, pre, refined, total, scal = call(
        coarse_kernel, [box] * 4 + [(1, 128)] * 2,
        [(2, 256, 128), (384, 256), ext, ext], 20, True,
    )(pos, gathered, r_ext, b, other_layers, x_high, x_low, other_xh, other_xl,
      y_high, y_low, other_yh, other_yl, wx, wy, wz, dg, iv, s, u)
    parts = gather_rows(total).reshape(NDEV, 128)
    direction, = call(finish_kernel, [box], [], 4)(parts, scal, refined, pre)
    return sol, res, direction


def solution(mesh):
    spec = P("gz", "gx", "gy")
    return jax.shard_map(
        local,
        mesh=mesh,
        in_specs=(spec, spec, spec, P(None, "gz", "gx", "gy")),
        out_specs=(spec, spec, spec),
        check_vma=False,
    )
```
